256 devices in a mesh: seq: 64 (over z, x, y_lo), kv: 4 (over y_hi, core).
Axes of the slice: x: 4, y: 4 (y_hi: 2, y_lo: 2; y = y_hi * 2 + y_lo), z: 8, core: 2. Of those that a mesh axis runs over, the one named last changes fastest.
Arguments:
- queries: bfloat16 [32768, 1024], P('seq'), may hold values from -88 to 88
- keys: bfloat16 [512, 64, 1024], P('seq', 'kv'), may hold values from -4 to 4
- values: bfloat16 [512, 64, 1024], P('seq', 'kv'), may hold values from -6 to 6
- layout: int32 [512, 71], replicated, may hold values from -1 to 511, as said below
- grad_out: bfloat16 [32768, 1024], P('seq'), may hold values from -6 to 6
Outputs:
- attended: bfloat16 [32768, 1024], P('seq')
- grad_q: bfloat16 [32768, 1024], P('seq')
- grad_k: bfloat16 [512, 64, 1024], P('seq', 'kv')
- grad_v: bfloat16 [512, 64, 1024], P('seq', 'kv')
The draws below stay inside these ranges and needn't reach their ends.
Inputs may be any that keep to these rules, and one draw needn't show every extreme that they name: `layout`: write query block b as 8 w + i with 0 <= i < 8. Row b lists the summary block of each window 0 .. w - 1 in order of windows, then the blocks 8 w .. 8 w + i in order, then -1 in the remaining entries. The summary block of window u is one of the blocks 8 u .. 8 u + 7 and is the same in every row.
All inputs are finite; a program needn't handle non-finite values.
Results may differ from the reference program's by a relative error of at most 0.038.
Values may be sent and summed in bfloat16 or wider, within the bound.
A program may use at most 128 MiB of HBM per device.

```python
import math
import jax
import jax.numpy as jnp
from jax import lax

HEADS = 8
HD = 128
BLK = 64
WB = 8
TOK_DEV = 512
DW = 1024
SEQ = 32768
NBLK = 512
KMAX = 71
N_SEQ = 64


def draw_queries(key, part):
    base = jnp.clip(jax.random.normal(jax.random.fold_in(key, 1), (SEQ, HEADS * HD), jnp.float32), -4.0, 4.0)
    return base.astype(jnp.bfloat16)


def draw_keys(key, part):
    base = jnp.clip(jax.random.normal(jax.random.fold_in(key, 2), (NBLK, BLK, HEADS * HD), jnp.float32), -4.0, 4.0)
    return base.astype(jnp.bfloat16)


def draw_layout(key, part):
    spot = jax.random.randint(jax.random.fold_in(key, 3), (N_SEQ,), 0, WB).astype(jnp.int32)
    summary = jnp.arange(N_SEQ, dtype=jnp.int32) * WB + spot
    block = jnp.arange(NBLK, dtype=jnp.int32)[:, None]
    entry = jnp.arange(KMAX, dtype=jnp.int32)[None, :]
    window = block // WB
    inner = block % WB
    earlier = summary[jnp.minimum(entry, N_SEQ - 1)]
    local_block = window * WB + entry - window
    listed = jnp.where(entry < window, earlier, jnp.where(entry <= window + inner, local_block, -1))
    return listed.astype(jnp.int32)


def block_scale(key, extent, split, least, top_value):
    def one(dim, shards_of):
        heights = jax.random.uniform(jax.random.fold_in(jax.random.fold_in(key, 6), dim), (shards_of,), jnp.float32, least / len(split), top_value / len(split))
        return jnp.repeat(jnp.exp(heights), extent[dim] // shards_of).reshape((-1,) + (1,) * (len(extent) - dim - 1))

    factor_of = one(*split[0])
    for cut in split[1:]:
        factor_of = factor_of * one(*cut)
    return factor_of


def centred(own_key, extent, width, reach, split=(), kind=jnp.bfloat16):
    drawn = width * jax.random.normal(own_key, extent, jnp.float32)
    if split:
        drawn = drawn * block_scale(own_key, extent, split, -0.22, 0.18)
    return jnp.clip(drawn, -reach, reach).astype(kind)


def setup_inputs(seed: int = 0) -> dict:
    key_list = jax.random.split(jax.random.key(seed), 6)
    return {
        "queries": draw_queries(jax.random.fold_in(key_list[5], 71), 0),
        "keys": draw_keys(jax.random.fold_in(key_list[5], 71), 0),
        "values": centred(key_list[2], (NBLK, BLK, DW), 1.0, 6.0, ((0, 64), (1, 4))),
        "layout": draw_layout(jax.random.fold_in(key_list[5], 71), 0),
        "grad_out": centred(key_list[4], (SEQ, DW), 1.0, 6.0, ((0, 64),)),
    }


def reference(queries, keys, values, layout, grad_out):
    score_scale = 1.0 / math.sqrt(HD)
    feat_width = HEADS * HD
    list_len = layout.shape[1]

    def window_step(carry, window):
        key_acc, value_acc = carry
        query_rows = lax.dynamic_slice_in_dim(queries, window * TOK_DEV, TOK_DEV, 0).astype(jnp.float32).reshape(WB, BLK, HEADS, HD)
        grad_rows = lax.dynamic_slice_in_dim(grad_out, window * TOK_DEV, TOK_DEV, 0).astype(jnp.float32).reshape(WB, BLK, HEADS, HD)
        entries = lax.dynamic_slice_in_dim(layout, window * WB, WB, 0)
        safe_idx = jnp.maximum(entries, 0).astype(jnp.int32)
        key_blocks = keys[safe_idx].astype(jnp.float32).reshape(WB, list_len, BLK, HEADS, HD)
        value_blocks = values[safe_idx].astype(jnp.float32).reshape(WB, list_len, BLK, HEADS, HD)
        own_block = (window * WB + jnp.arange(WB, dtype=jnp.int32)).astype(jnp.int32)[:, None]
        token_pos = jnp.arange(BLK, dtype=jnp.int32)
        causal = token_pos[None, :] <= token_pos[:, None]
        earlier = (entries >= 0) & (entries < own_block)
        same = entries == own_block
        pair_ok = earlier[:, None, :, None] | same[:, None, :, None] & causal[None, :, None, :]
        valid_pair = pair_ok[:, None]
        raw_score = jnp.einsum('bihd,bkjhd->bhikj', query_rows, key_blocks) * score_scale
        row_peak = lax.optimization_barrier(jnp.max(jnp.where(valid_pair, raw_score, -jnp.inf), axis=(3, 4), keepdims=True))
        weight = jnp.where(valid_pair, jnp.exp(raw_score - row_peak), 0.0)
        row_total = lax.optimization_barrier(jnp.sum(weight, axis=(3, 4), keepdims=True))
        weight_b = lax.optimization_barrier(weight.astype(jnp.bfloat16)).astype(jnp.float32)
        out_sum = jnp.einsum('bhikj,bkjhd->bihd', weight_b, value_blocks)
        total_rows = jnp.transpose(row_total[:, :, :, 0, 0], (0, 2, 1))[..., None]
        attended = (out_sum / total_rows).astype(jnp.bfloat16)
        att_f = attended.astype(jnp.float32)
        row_delta = lax.optimization_barrier(jnp.sum(grad_rows * att_f, axis=3))
        prob = jnp.where(valid_pair, jnp.exp(raw_score - row_peak) / row_total, 0.0)
        grad_prob = jnp.einsum('bihd,bkjhd->bhikj', grad_rows, value_blocks)
        delta_wide = jnp.transpose(row_delta, (0, 2, 1))[:, :, :, None, None]
        grad_score = score_scale * prob * (grad_prob - delta_wide)
        grad_score = lax.optimization_barrier(grad_score.astype(jnp.bfloat16)).astype(jnp.float32)
        prob_b = lax.optimization_barrier(prob.astype(jnp.bfloat16)).astype(jnp.float32)
        query_grad = jnp.einsum('bhikj,bkjhd->bihd', grad_score, key_blocks)
        key_grad = jnp.einsum('bhikj,bihd->bkjhd', grad_score, query_rows)
        value_grad = jnp.einsum('bhikj,bihd->bkjhd', prob_b, grad_rows)
        flat_idx = safe_idx.reshape(-1)
        key_acc = key_acc.at[flat_idx].add(key_grad.reshape(WB * list_len, BLK, feat_width))
        value_acc = value_acc.at[flat_idx].add(value_grad.reshape(WB * list_len, BLK, feat_width))
        outputs = (attended.reshape(TOK_DEV, feat_width), query_grad.astype(jnp.bfloat16).reshape(TOK_DEV, feat_width))
        return ((key_acc, value_acc), outputs)
    start_acc = (jnp.zeros((NBLK, BLK, feat_width), jnp.float32), jnp.zeros((NBLK, BLK, feat_width), jnp.float32))
    (key_acc, value_acc), (att_all, qgrad_all) = lax.scan(window_step, start_acc, jnp.arange(N_SEQ, dtype=jnp.int32))
    attended = att_all.reshape(SEQ, feat_width)
    grad_q = qgrad_all.reshape(SEQ, feat_width)
    return (attended, grad_q, key_acc.astype(jnp.bfloat16), value_acc.astype(jnp.bfloat16))
```

```python
import functools
import math

import jax
import jax.numpy as jnp
from jax import lax
from jax.experimental import pallas as pl
from jax.experimental.pallas import tpu as pltpu
from jax.sharding import PartitionSpec as P

HD = 128
PLANE = 8
MESH = pl.DeviceIdType.MESH
F32 = jnp.float32
BF16 = jnp.bfloat16
SCALE = 1.0 / math.sqrt(HD)
LOG2_SCALE = math.log2(math.e) / math.sqrt(HD)
NT = (((1,), (1,)), ((), ()))
NN = (((1,), (0,)), ((), ()))
TN = (((0,), (0,)), ((), ()))
KEY_TILE = 256


def dot(a, b, dims):
    return lax.dot_general(a, b, dims, preferred_element_type=F32)


def kernel(
    nz, layout_ref, q_hbm, k_in, v_in, do_hbm,
    att_out, dq_out, dk_out, dv_out,
    q, do, sums, ag, grad, m, l, acc, lse_row, delta_row, dqt, att, dq, fin,
    sk1, sk2, sk3, sv1, sv2, sv3, sz, rk1, rk2, rk3, rv1, rv2, rv3, rz, own,
    load_sem, sum_s, sum_r, kv_s, kv_r, zs, zr, ag_s, ag_r, rs_s, rs_r, gz_s, gz_r,
    att_s, att_r, dq_s, dq_r, fin_s, fin_r, loc_sem,
):
    tok, width = q.shape
    heads = width // HD
    blocks, part_tok = k_in.shape[0], k_in.shape[1]
    blk = ag.shape[3]
    half = blk // 2
    n_kv = lax.axis_size("kv")
    s = lax.axis_index("seq")
    k = lax.axis_index("kv")
    z, r = s // PLANE, s % PLANE
    x, y = r // 2, r % 2
    left, right, opp, yo = (x + 3) % 4, (x + 1) % 4, (x + 2) % 4, 1 - y
    base = z * PLANE
    dev_left = {"seq": base + left * 2 + y}
    dev_right = {"seq": base + right * 2 + y}
    dev_y = {"seq": base + x * 2 + yo}
    peers = [(k + i) % n_kv for i in range(1, n_kv)]
    cols = pl.ds(pl.multiple_of(k * width, width), width)

    def peer_cols(p):
        return pl.ds(pl.multiple_of(p * width, width), width)

    def part(p):
        return pl.ds(pl.multiple_of(p * part_tok, part_tok), part_tok)

    def rcopy(src, dst, send, recv, dev):
        return pltpu.make_async_remote_copy(
            src_ref=src, dst_ref=dst, send_sem=send, recv_sem=recv, device_id=dev, device_id_type=MESH
        )

    load_q = pltpu.make_async_copy(q_hbm.at[:, cols], q, load_sem.at[0])
    load_do = pltpu.make_async_copy(do_hbm.at[:, cols], do, load_sem.at[1])
    load_q.start()
    load_do.start()
    barrier = pltpu.get_barrier_semaphore()
    for p in peers:
        pl.semaphore_signal(barrier, inc=1, device_id={"kv": p}, device_id_type=MESH)
    for dev in (dev_left, dev_right, dev_y):
        pl.semaphore_signal(barrier, inc=1, device_id=dev, device_id_type=MESH)
    for i in range(1, nz):
        pl.semaphore_signal(
            barrier, inc=1, device_id={"seq": ((z + i) % nz) * PLANE + r}, device_id_type=MESH
        )
    summary = jnp.clip(
        layout_ref[layout_ref.shape[0] - 1, jnp.minimum(s, nz * PLANE - 2)] - s * blocks, 0, blocks - 1
    )
    sums[0] = k_in[summary]
    sums[1] = v_in[summary]
    pl.semaphore_wait(barrier, len(peers) + 3 + nz - 1)

    def sum_copy(p, slot):
        return rcopy(
            sums.at[:, :, peer_cols(p)], ag.at[z, :, r, part(slot)], sum_s.at[p], sum_r.at[slot], {"kv": p}
        )

    for p in peers:
        sum_copy(p, k).start()
    own_sum = pltpu.make_async_copy(sums.at[:, :, cols], ag.at[z, :, r, part(k)], loc_sem.at[0])
    own_sum.start()

    def kv_copy(t, p, slot):
        ref = (k_in, v_in)[t]
        return rcopy(
            ref.at[:, :, peer_cols(p)], ag.at[nz, t, :, part(slot)], kv_s.at[t, p], kv_r.at[t, slot], {"kv": p}
        )

    own_kv = [
        pltpu.make_async_copy(ref.at[:, :, cols], ag.at[nz, t, :, part(k)], loc_sem.at[1 + t])
        for t, ref in enumerate((k_in, v_in))
    ]
    for c in own_kv:
        c.start()
    own_sum.wait()
    for p in peers:
        sum_copy(p, p).wait_recv()

    def z_copy(dz):
        return rcopy(ag.at[z, :, r], ag.at[z, :, r], zs.at[dz], zr.at[z], {"seq": s + dz * PLANE})

    for dz in range(1, nz):
        @pl.when(z + dz < nz)
        def _(dz=dz):
            z_copy(dz).start()

    for t in range(2):
        for p in peers:
            kv_copy(t, p, k).start()

    def blk_x(o, t, xx, yy):
        return ag.at[o, t, xx * 2 + yy]

    def pair(o, xx):
        return ag.at[o, 0, pl.ds(xx * 2, 2)]

    def agc(o, i, ref, dev, j=None):
        j = i if j is None else j
        return rcopy(ref, ref, ag_s.at[o, i], ag_r.at[o, j], dev)

    def lo(ref):
        return ref.at[pl.ds(0, half)]

    def hi(ref):
        return ref.at[pl.ds(half, half)]

    def ag1(o):
        return [
            agc(o, 0, blk_x(o, 0, x, y), dev_y),
            agc(o, 1, blk_x(o, 1, x, y), dev_right),
            agc(o, 2, blk_x(o, 1, x, y), dev_left),
            agc(o, 3, blk_x(o, 1, x, y), dev_y, 10 + x),
        ]

    def ag1_in(o):
        return [
            agc(o, 0, blk_x(o, 0, x, yo), dev_y),
            agc(o, 1, blk_x(o, 1, left, y), dev_left),
            agc(o, 2, blk_x(o, 1, right, y), dev_right),
        ]

    def ag2(o):
        return [
            agc(o, 4, pair(o, x), dev_right),
            agc(o, 5, pair(o, x), dev_left),
            agc(o, 6, lo(blk_x(o, 1, left, y)), dev_right),
            agc(o, 7, hi(blk_x(o, 1, right, y)), dev_left),
            agc(o, 8, blk_x(o, 1, left, y), dev_y, 10 + left),
            agc(o, 9, blk_x(o, 1, right, y), dev_y, 10 + right),
        ]

    def ag2_in(o):
        return [
            agc(o, 4, pair(o, left), dev_left),
            agc(o, 5, pair(o, right), dev_right),
            agc(o, 6, lo(blk_x(o, 1, opp, y)), dev_left),
            agc(o, 7, hi(blk_x(o, 1, opp, y)), dev_right),
        ]

    def ag3(o):
        return [
            agc(o, 10, blk_x(o, 0, left, 0), dev_right, 8),
            agc(o, 11, blk_x(o, 0, right, 1), dev_left, 9),
            agc(o, 12, blk_x(o, 1, opp, y), dev_y, 10 + opp),
        ]

    def ag3_in(o):
        return [
            agc(o, 8, blk_x(o, 0, opp, 0), dev_left),
            agc(o, 9, blk_x(o, 0, opp, 1), dev_right),
        ] + [agc(o, 0, blk_x(o, 1, xx, yo), dev_y, 10 + xx) for xx in range(4)]

    def start(copies):
        for c in copies:
            c.start()

    def recv(copies):
        for c in copies:
            c.wait_recv()

    def sent(copies):
        for c in copies:
            c.wait_send()

    m[...] = jnp.full_like(m, -1e30)
    l[...] = jnp.zeros_like(l)
    acc[...] = jnp.zeros_like(acc)
    load_q.wait()
    load_do.wait()

    plane_keys = PLANE * blk

    def forward(c, slope, offset, masked):
        if masked:
            row = lax.broadcasted_iota(jnp.int32, (tok, 1), 0) * slope + offset
            lane = lax.broadcasted_iota(jnp.int32, (tok, HD), 1)
        for h in range(heads):
            hs = slice(h * HD, h * HD + HD)
            kk = ag[c, 0, :, :, hs].reshape(plane_keys, HD)
            vv = ag[c, 1, :, :, hs].reshape(plane_keys, HD)
            score = dot(q[:, hs], kk, NT) * LOG2_SCALE
            tiles = [score[:, j * HD : j * HD + HD] for j in range(plane_keys // HD)]
            if masked:
                tiles = [jnp.where(lane + j * HD <= row, t, -jnp.inf) for j, t in enumerate(tiles)]
            top = functools.reduce(jnp.maximum, tiles)
            m_old = m[h]
            m_new = jnp.maximum(m_old, jnp.max(top, axis=1, keepdims=True))
            alpha = jnp.exp2(m_old - m_new)
            weights = [jnp.exp2(t - m_new) for t in tiles]
            l[h] = l[h] * alpha + functools.reduce(jnp.add, weights)
            w = jnp.concatenate([t.astype(BF16) for t in weights], axis=1)
            acc[h] = acc[h] * alpha + dot(w, vv, NN)
            m[h] = m_new

    def fwd_step(it, _):
        @pl.when(it <= z)
        def _():
            o = z - it

            @pl.when(it > 0)
            def _():
                rcopy(ag.at[o, :, r], ag.at[o, :, r], zs.at[0], zr.at[o], dev_y).wait_recv()

            start(ag1(o))

        @pl.when((it >= 1) & (it - 1 <= z))
        def _():
            o = z - (it - 1)
            recv(ag1_in(o))
            start(ag2(o))

        @pl.when((it >= 2) & (it - 2 <= z))
        def _():
            o = z - (it - 2)
            recv(ag2_in(o))
            start(ag3(o))

        @pl.when(it == 0)
        def _():
            for c in own_kv:
                c.wait()
            for t in range(2):
                for p in peers:
                    kv_copy(t, p, p).wait_recv()

        @pl.when(it >= 3)
        def _():
            recv(ag3_in(z - (it - 3)))

        @pl.when((it == 0) | (it == 3))
        def _():
            local = it == 0
            forward(
                jnp.where(local, nz, z), jnp.where(local, 1, 0), jnp.where(local, 0, r * blk - 1), True
            )

        @pl.when(it > 3)
        def _():
            forward(z - (it - 3), 0, 0, False)

        return 0

    lax.fori_loop(0, z + 4, fwd_step, 0)

    for h in range(heads):
        hs = slice(h * HD, h * HD + HD)
        total = jnp.sum(l[h], axis=1, keepdims=True)
        out = (acc[h] / total).astype(BF16)
        att[:, hs] = out
        delta = jnp.sum(out.astype(F32) * do[:, hs].astype(F32), axis=1, keepdims=True)
        lse_row[h] = jnp.transpose(m[h] + jnp.log2(total))[:8]
        delta_row[h] = jnp.transpose(jnp.broadcast_to(delta, (tok, HD)))[:8]

    def out_copy(src, dst, send, recv_, p, slot):
        return rcopy(src, dst.at[:, peer_cols(slot)], send.at[p], recv_.at[slot], {"kv": p})

    for p in peers:
        out_copy(att, att_out, att_s, att_r, p, k).start()
    own_att = pltpu.make_async_copy(att, att_out.at[:, cols], loc_sem.at[3])
    own_att.start()

    dqt[...] = jnp.zeros_like(dqt)

    def backward(c, slope, offset, masked):
        tile_blocks = KEY_TILE // blk
        for h in range(heads):
            hs = slice(h * HD, h * HD + HD)
            lse = lse_row[h, 0:1, :]
            delta = delta_row[h, 0:1, :]
            qh, doh = q[:, hs], do[:, hs]
            for t in range(plane_keys // KEY_TILE):
                bs = slice(t * tile_blocks, (t + 1) * tile_blocks)
                kk = ag[c, 0, bs, :, hs].reshape(KEY_TILE, HD)
                vv = ag[c, 1, bs, :, hs].reshape(KEY_TILE, HD)
                prob = jnp.exp2(dot(kk, qh, NT) * LOG2_SCALE - lse)
                if masked:
                    row = lax.broadcasted_iota(jnp.int32, (1, tok), 1) * slope + offset
                    key = lax.broadcasted_iota(jnp.int32, (KEY_TILE, tok), 0) + t * KEY_TILE
                    prob = jnp.where(key <= row, prob, 0.0)
                ds = (prob * (dot(vv, doh, NT) - delta)).astype(BF16)
                grad[c, 1, bs, :, hs] = dot(prob.astype(BF16), doh, NN).reshape(tile_blocks, blk, HD)
                grad[c, 0, bs, :, hs] = (dot(ds, qh, NN) * SCALE).reshape(tile_blocks, blk, HD)
                dqt[h] += dot(kk, ds, TN)

    def rsc(o, i, src, dst, dev):
        return rcopy(src, dst, rs_s.at[o, i], rs_r.at[o, i], dev)

    def rs1(o):
        return [
            rsc(o, 0, sk1.at[o, 0], rk1.at[o, 0], dev_left),
            rsc(o, 1, sk1.at[o, 1], rk1.at[o, 1], dev_right),
            rsc(o, 2, sv1.at[o], rv1.at[o], dev_y),
        ]

    def rs2(o):
        return [
            rsc(o, 3, sk2.at[o, 0], rk2.at[o, 0], dev_left),
            rsc(o, 4, sk2.at[o, 1], rk2.at[o, 1], dev_right),
            rsc(o, 5, sv2.at[o, 0], rv2.at[o, 0], dev_left),
            rsc(o, 6, sv2.at[o, 1], rv2.at[o, 1], dev_right),
        ]

    def rs3(o):
        return [
            rsc(o, 7, sk3.at[o], rk3.at[o], dev_y),
            rsc(o, 8, sv3.at[o, 0], rv3.at[o, 0], dev_left),
            rsc(o, 9, sv3.at[o, 1], rv3.at[o, 1], dev_right),
        ]

    def gz_copy(o):
        return rcopy(sz.at[o], rz.at[z], gz_s.at[o], gz_r.at[z], {"seq": o * PLANE + r})

    def reduce1(o):
        sk1[o, 0] = grad[o, 0, opp * 2].astype(BF16)
        sk1[o, 1] = grad[o, 0, opp * 2 + 1].astype(BF16)
        for xx in range(4):
            sv1[o, xx] = grad[o, 1, xx * 2 + yo].astype(BF16)
        start(rs1(o))

    def reduce2(o):
        recv(rs1(o))
        sk2[o, 0, 0] = (grad[o, 0, left * 2] + rk1[o, 0].astype(F32)).astype(BF16)
        sk2[o, 0, 1] = grad[o, 0, left * 2 + 1].astype(BF16)
        sk2[o, 1, 0] = grad[o, 0, right * 2].astype(BF16)
        sk2[o, 1, 1] = (grad[o, 0, right * 2 + 1] + rk1[o, 1].astype(F32)).astype(BF16)
        for xx in range(4):
            grad[o, 1, xx * 2 + y] += rv1[o, xx].astype(F32)
        far = grad[o, 1, opp * 2 + y].astype(BF16)
        sv2[o, 0] = far[:half]
        sv2[o, 1] = far[half:]
        start(rs2(o))

    def reduce3(o):
        recv(rs2(o))
        for yy in range(2):
            grad[o, 0, x * 2 + yy] += rk2[o, 0, yy].astype(F32) + rk2[o, 1, yy].astype(F32)
        sk3[o] = grad[o, 0, x * 2 + yo].astype(BF16)
        sv3[o, 0, :half] = (grad[o, 1, left * 2 + y, :half] + rv2[o, 0].astype(F32)).astype(BF16)
        sv3[o, 0, half:] = grad[o, 1, left * 2 + y, half:].astype(BF16)
        sv3[o, 1, :half] = grad[o, 1, right * 2 + y, :half].astype(BF16)
        sv3[o, 1, half:] = (grad[o, 1, right * 2 + y, half:] + rv2[o, 1].astype(F32)).astype(BF16)
        start(rs3(o))

    def reduce4(o):
        recv(rs3(o))
        own[0] = grad[o, 0, r] + rk3[o].astype(F32)
        own[1] = grad[o, 1, r] + (rv3[o, 0].astype(F32) + rv3[o, 1].astype(F32))

        @pl.when(o < z)
        def _():
            sz[o] = own[...].astype(BF16)
            gz_copy(o).start()

    def bwd_step(it, _):
        @pl.when(it < z)
        def _():
            backward(it, 0, 0, False)

        @pl.when((it == z) | (it == z + 1))
        def _():
            local = it > z
            backward(
                jnp.where(local, nz, z), jnp.where(local, 1, 0), jnp.where(local, 0, r * blk - 1), True
            )

        @pl.when(it <= z)
        def _():
            reduce1(it)

        @pl.when(it == z + 1)
        def _():
            for h in range(heads):
                hs = slice(h * HD, h * HD + HD)
                dq[:, hs] = jnp.transpose(dqt[h] * SCALE).astype(BF16)
            for p in peers:
                out_copy(dq, dq_out, dq_s, dq_r, p, k).start()
            pltpu.make_async_copy(dq, dq_out.at[:, cols], loc_sem.at[4]).start()

        @pl.when(it >= 3)
        def _():
            reduce4(it - 3)

        @pl.when((it >= 2) & (it - 2 <= z))
        def _():
            reduce3(it - 2)

        @pl.when((it >= 1) & (it - 1 <= z))
        def _():
            reduce2(it - 1)

        return 0

    lax.fori_loop(0, z + 4, bwd_step, 0)

    def add_plane(o, _):
        rcopy(sz.at[0], rz.at[o], gz_s.at[0], gz_r.at[o], dev_y).wait_recv()
        own[...] += rz[o].astype(F32)
        return 0

    lax.fori_loop(z + 1, nz, add_plane, 0)
    for t in range(2):
        for b in range(blocks):
            chosen = jnp.where(summary == b, own[t], 0.0)
            fin[t, b] = (grad[nz, t, b] + chosen).astype(BF16)

    def fin_copy(t, p, slot):
        out = (dk_out, dv_out)[t]
        return rcopy(
            fin.at[t, :, part(p)], out.at[:, :, peer_cols(slot)], fin_s.at[t, p], fin_r.at[t, slot], {"kv": p}
        )

    own_fin = [
        pltpu.make_async_copy(fin.at[t, :, part(k)], ref.at[:, :, cols], loc_sem.at[5 + t])
        for t, ref in enumerate((dk_out, dv_out))
    ]
    for t in range(2):
        for p in peers:
            fin_copy(t, p, k).start()
        own_fin[t].start()

    for p in peers:
        sum_copy(p, k).wait_send()
        for t in range(2):
            kv_copy(t, p, k).wait_send()
    for dz in range(1, nz):
        @pl.when(z + dz < nz)
        def _(dz=dz):
            z_copy(dz).wait_send()

    def sent_step(o, _):
        sent(ag1(o) + ag2(o) + ag3(o) + rs1(o) + rs2(o) + rs3(o))

        @pl.when(o < z)
        def _():
            gz_copy(o).wait_send()

        return 0

    lax.fori_loop(0, z + 1, sent_step, 0)
    own_att.wait()
    pltpu.make_async_copy(dq, dq_out.at[:, cols], loc_sem.at[4]).wait()
    for p in peers:
        for src, dst, send, recv_ in ((att, att_out, att_s, att_r), (dq, dq_out, dq_s, dq_r)):
            out_copy(src, dst, send, recv_, p, k).wait_send()
            out_copy(src, dst, send, recv_, p, p).wait_recv()
    for t in range(2):
        own_fin[t].wait()
        for p in peers:
            fin_copy(t, p, k).wait_send()
            fin_copy(t, p, p).wait_recv()


def shards(queries, keys, values, layout, grad_out):
    tok, feat = queries.shape
    blocks, part_tok = keys.shape[0], keys.shape[1]
    n_kv = lax.axis_size("kv")
    nz = lax.axis_size("seq") // PLANE
    blk = part_tok * n_kv
    width = feat // n_kv
    heads = width // HD
    rows, entries = layout.shape
    any_spec = pl.BlockSpec(memory_space=pl.ANY)
    whole = pl.BlockSpec(keys.shape, lambda i: (0, 0, 0))
    dma = pltpu.SemaphoreType.DMA

    def vm(*shape, dtype=BF16):
        return pltpu.VMEM(shape, dtype)

    half = blk // 2
    return pl.pallas_call(
        functools.partial(kernel, nz),
        grid=(1,),
        out_shape=(
            jax.ShapeDtypeStruct(queries.shape, BF16),
            jax.ShapeDtypeStruct(queries.shape, BF16),
            jax.ShapeDtypeStruct(keys.shape, BF16),
            jax.ShapeDtypeStruct(keys.shape, BF16),
        ),
        in_specs=[
            pl.BlockSpec((8, entries), lambda i: (rows // 8 - 1, 0), memory_space=pltpu.SMEM),
            any_spec,
            whole,
            whole,
            any_spec,
        ],
        out_specs=[any_spec] * 4,
        scratch_shapes=[
            vm(tok, width),
            vm(tok, width),
            vm(2, part_tok, feat),
            vm(nz + 1, 2, PLANE, blk, width),
            vm(nz + 1, 2, PLANE, blk, width, dtype=F32),
            vm(heads, tok, HD, dtype=F32),
            vm(heads, tok, HD, dtype=F32),
            vm(heads, tok, HD, dtype=F32),
            vm(heads, 8, tok, dtype=F32),
            vm(heads, 8, tok, dtype=F32),
            vm(heads, HD, tok, dtype=F32),
            vm(tok, width),
            vm(tok, width),
            vm(2, blocks, blk, width),
            vm(nz, 2, blk, width),
            vm(nz, 2, 2, blk, width),
            vm(nz, blk, width),
            vm(nz, 4, blk, width),
            vm(nz, 2, half, width),
            vm(nz, 2, blk, width),
            vm(nz, 2, blk, width),
            vm(nz, 2, blk, width),
            vm(nz, 2, 2, blk, width),
            vm(nz, blk, width),
            vm(nz, 4, blk, width),
            vm(nz, 2, half, width),
            vm(nz, 2, blk, width),
            vm(nz, 2, blk, width),
            vm(2, blk, width, dtype=F32),
            dma((2,)),
            dma((n_kv,)),
            dma((n_kv,)),
            dma((2, n_kv)),
            dma((2, n_kv)),
            dma((nz,)),
            dma((nz,)),
            dma((nz, 13)),
            dma((nz, 14)),
            dma((nz, 10)),
            dma((nz, 10)),
            dma((nz,)),
            dma((nz,)),
            dma((n_kv,)),
            dma((n_kv,)),
            dma((n_kv,)),
            dma((n_kv,)),
            dma((2, n_kv)),
            dma((2, n_kv)),
            dma((7,)),
        ],
        compiler_params=pltpu.CompilerParams(
            collective_id=0, has_side_effects=True, vmem_limit_bytes=58 * 1024 * 1024
        ),
    )(layout, queries, keys, values, grad_out)


def solution(mesh):
    return jax.shard_map(
        shards,
        mesh=mesh,
        in_specs=(P("seq", None), P("seq", "kv", None), P("seq", "kv", None), P(), P("seq", None)),
        out_specs=(P("seq", None), P("seq", None), P("seq", "kv", None), P("seq", "kv", None)),
        check_vma=False,
    )
```

```python
import functools
import math

import jax
import jax.numpy as jnp
from jax import lax
from jax.experimental import pallas as pl
from jax.experimental.pallas import tpu as pltpu
from jax.sharding import PartitionSpec as P

HD = 128
PLANE = 8
MESH = pl.DeviceIdType.MESH
F32 = jnp.float32
BF16 = jnp.bfloat16
SCALE = 1.0 / math.sqrt(HD)
LOG2_SCALE = math.log2(math.e) / math.sqrt(HD)
NT = (((1,), (1,)), ((), ()))
NN = (((1,), (0,)), ((), ()))
TN = (((0,), (0,)), ((), ()))
KEY_TILE = 256
LAG = 2
VMEM_LIMIT = 123 * 512 * 1024


def dot(a, b, dims):
    return lax.dot_general(a, b, dims, preferred_element_type=F32)


def kernel(
    nz, layout_hbm, q_hbm, k_hbm, v_hbm, do_hbm,
    att_out, dq_out, dk_out, dv_out,
    lay, k_in, v_in, q, do, sums, ag, grad, m, l, acc, lse_row, delta_row, dqt, att, dq, fin, fin_in, tail, tail_in, res,
    s0, s1, s2, s3, sz, szl, r0, r1, r2, r3, rz, rzl, own,
    load_sem, sum_s, sum_r, kv_s, kv_r, zs, zr, zl_s, zl_r, ag_s, ag_r, rs_s, rs_r, gz_s, gz_r,
    gl_s, gl_r, att_s, att_r, dq_s, dq_r, fin_s, fin_r, tail_s, tail_r, first_s, first_r, d0_s, d0_r, loc_sem,
):
    heads, tok, _ = q.shape
    width = heads * HD
    blocks, part_tok = k_in.shape[0], k_in.shape[1]
    blk = ag.shape[4]
    n_kv = lax.axis_size("kv")
    s = lax.axis_index("seq")
    k = lax.axis_index("kv")
    z, r = s // PLANE, s % PLANE
    x, y = r // 2, r % 2
    left, right, opp, yo = (x + 3) % 4, (x + 1) % 4, (x + 2) % 4, 1 - y
    base = z * PLANE
    dev_left = {"seq": base + left * 2 + y}
    dev_right = {"seq": base + right * 2 + y}
    dev_y = {"seq": base + x * 2 + yo}
    dev_up = {"seq": s + PLANE}
    dev_down = {"seq": s - PLANE}
    dev_top = {"seq": (nz - 1) * PLANE + r}
    dev_bottom = {"seq": r}
    has_up, has_down = z + 1 < nz, z > 0
    wrap = nz > 2
    is_bottom, is_top = z == 0, z == nz - 1
    peers = [(k + i) % n_kv for i in range(1, n_kv)]
    sibling = (k // 2) * 2 + (k + 1) % 2
    across = (k + 2) % n_kv
    corner = (sibling + 2) % n_kv
    far = jnp.maximum(0, jnp.minimum(z, nz - 2) - 1)
    done = 3 * LAG - 1
    ends = [far + done, jnp.maximum(2 * far + done, far + done + 1)]
    bwd_at = ends[0] + 1

    def peer_cols(p):
        return pl.ds(pl.multiple_of(p * width, width), width)

    cols = peer_cols(k)

    def head_cols(p, h):
        return pl.ds(pl.multiple_of(p * width + h * HD, HD), HD)

    def part(p):
        return pl.ds(pl.multiple_of(p * part_tok, part_tok), part_tok)

    def rcopy(src, dst, send, recv, dev):
        return pltpu.make_async_remote_copy(
            src_ref=src, dst_ref=dst, send_sem=send, recv_sem=recv, device_id=dev, device_id_type=MESH
        )

    barrier = pltpu.get_barrier_semaphore()
    for p in peers:
        pl.semaphore_signal(barrier, inc=1, device_id={"kv": p}, device_id_type=MESH)
    mates = [(r + i) % PLANE for i in range(1, PLANE)]
    for w in mates:
        pl.semaphore_signal(barrier, inc=1, device_id={"seq": base + w}, device_id_type=MESH)
    for i in range(1, nz):
        pl.semaphore_signal(
            barrier, inc=1, device_id={"seq": ((z + i) % nz) * PLANE + r}, device_id_type=MESH
        )
    loads = [
        pltpu.make_async_copy(src, dst, load_sem.at[i])
        for i, (src, dst) in enumerate(
            (
                (layout_hbm.at[:, pl.ds(layout_hbm.shape[1] - lay.shape[1], lay.shape[1])], lay),
                (k_hbm, k_in),
                (v_hbm, v_in),
                *((q_hbm.at[:, head_cols(k, h)], q.at[h]) for h in range(heads)),
                *((do_hbm.at[:, head_cols(k, h)], do.at[h]) for h in range(heads)),
            )
        )
    ]
    for c in loads:
        c.start()
    for c in loads[:3]:
        c.wait()
    entry = lax.broadcasted_iota(jnp.int32, (lay.shape[0], 1), 0)
    last_row = lay[:, lay.shape[1] - 1 :]
    named = jnp.where(entry == jnp.minimum(s, nz * PLANE - 2), last_row, 0)
    summary = jnp.clip(jnp.sum(named, axis=0, keepdims=True) - s * blocks, 0, blocks - 1)
    for t, ref in enumerate((k_in, v_in)):
        picked = ref[0]
        for b in range(1, blocks):
            picked = jnp.where(summary == b, ref[b], picked)
        for h in range(n_kv * heads):
            sums[h, t] = picked[:, h * HD : h * HD + HD]
    pl.semaphore_wait(barrier, len(peers) + PLANE - 1 + nz - 1)

    def sum_copy(p, slot):
        return rcopy(
            sums.at[pl.ds(p * heads, heads)],
            ag.at[z, :, :, r, part(slot)],
            sum_s.at[p],
            sum_r.at[slot],
            {"kv": p},
        )

    for p in peers:
        sum_copy(p, k).start()
    own_sum = pltpu.make_async_copy(
        sums.at[pl.ds(k * heads, heads)], ag.at[z, :, :, r, part(k)], loc_sem.at[0]
    )
    own_sum.start()

    def kv_copies(p, slot):
        return [
            rcopy(
                ref.at[:, :, head_cols(p, h)],
                ag.at[nz, h, t, :, part(slot)],
                kv_s.at[h, t, p],
                kv_r.at[h, t, slot],
                {"kv": p},
            )
            for h in range(heads)
            for t, ref in enumerate((k_in, v_in))
        ]

    own_kv = [
        pltpu.make_async_copy(
            ref.at[:, :, head_cols(k, h)], ag.at[nz, h, t, :, part(k)], loc_sem.at[1 + 2 * h + t]
        )
        for h in range(heads)
        for t, ref in enumerate((k_in, v_in))
    ]
    for c in own_kv:
        c.start()
    own_sum.wait()
    for p in peers:
        sum_copy(p, p).wait_recv()


    def agc(o, h, i, ref, dev):
        return rcopy(ref, ref, ag_s.at[o, h, i], ag_r.at[o, h, i], dev)

    def block(o, h, xx, yy):
        return ag.at[o, h, :, xx * 2 + yy]

    def pair(o, h, xx):
        return ag.at[o, h, :, pl.ds(xx * 2, 2)]

    def pair_of(o, h, t, xx):
        return ag.at[o, h, t, pl.ds(xx * 2, 2)]

    def ag1(o, h):
        return [agc(o, h, 0, block(o, h, x, y), dev_y)]

    def ag1_in(o, h):
        return [agc(o, h, 0, block(o, h, x, yo), dev_y)]

    def ag2(o, h):
        return [agc(o, h, 1, pair(o, h, x), dev_right), agc(o, h, 2, pair(o, h, x), dev_left)]

    def ag2_in(o, h):
        return [agc(o, h, 1, pair(o, h, left), dev_left), agc(o, h, 2, pair(o, h, right), dev_right)]

    def ag3(o, h):
        return [
            agc(o, h, 3, pair_of(o, h, 0, left), dev_right),
            agc(o, h, 4, pair_of(o, h, 1, right), dev_left),
        ]

    def ag3_in(o, h):
        return [
            agc(o, h, 3, pair_of(o, h, 0, opp), dev_left),
            agc(o, h, 4, pair_of(o, h, 1, opp), dev_right),
        ]

    def start(copies):
        for c in copies:
            c.start()

    def recv(copies):
        for c in copies:
            c.wait_recv()

    def sent(copies):
        for c in copies:
            c.wait_send()

    def z_copy(dz, h):
        return rcopy(ag.at[z, h, :, r], ag.at[z, h, :, r], zs.at[dz, h], zr.at[z, h], {"seq": s + dz * PLANE})

    def up_copy(o, h):
        return rcopy(ag.at[o, h], ag.at[o, h], zl_s.at[0, h], zl_r.at[0, h], dev_up)

    def wrap_copy(o, h):
        return rcopy(ag.at[o, h], ag.at[o, h], zl_s.at[1, h], zl_r.at[1, h], dev_top)

    def first_copy(w, slot):
        ref = ag.at[z, :, :, slot]
        return rcopy(ref, ref, first_s.at[w], first_r.at[slot], {"seq": base + w})

    for w in mates:
        first_copy(w, r).start()
    for h in range(heads):
        for dz in range(2, nz - 1):
            @pl.when(z + dz < nz)
            def _(dz=dz, h=h):
                z_copy(dz, h).start()

    for p in peers:
        start(kv_copies(p, k))
    m[...] = jnp.full_like(m, -1e30)
    l[...] = jnp.zeros_like(l)
    acc[...] = jnp.zeros_like(acc)
    dqt[...] = jnp.zeros_like(dqt)
    for c in loads[3:]:
        c.wait()
    for w in mates:
        first_copy(w, w).wait_recv()
    for h in range(heads):
        @pl.when(has_up)
        def _(h=h):
            up_copy(z, h).start()

        if wrap:
            @pl.when(is_bottom)
            def _(h=h):
                wrap_copy(z, h).start()

    plane_keys = PLANE * blk

    def forward(c, h, slope, offset, masked):
        kk = ag[c, h, 0].reshape(plane_keys, HD)
        vv = ag[c, h, 1].reshape(plane_keys, HD)
        score = dot(q[h], kk, NT) * LOG2_SCALE
        tiles = [score[:, j * HD : j * HD + HD] for j in range(plane_keys // HD)]
        if masked:
            row = lax.broadcasted_iota(jnp.int32, (tok, 1), 0) * slope + offset
            lane = lax.broadcasted_iota(jnp.int32, (tok, HD), 1)
            tiles = [jnp.where(lane + j * HD <= row, t, -jnp.inf) for j, t in enumerate(tiles)]
        top = functools.reduce(jnp.maximum, tiles)
        m_old = m[h]
        m_new = jnp.maximum(m_old, jnp.max(top, axis=1, keepdims=True))
        alpha = jnp.exp2(m_old - m_new)
        weights = [jnp.exp2(t - m_new) for t in tiles]
        l[h] = l[h] * alpha + functools.reduce(jnp.add, weights)
        w = jnp.concatenate([t.astype(BF16) for t in weights], axis=1)
        acc[h] = acc[h] * alpha + dot(w, vv, NN)
        m[h] = m_new

    def out_copy(src, dst, send, recv_, i, p, slot, h):
        return rcopy(
            src.at[h], dst.at[:, head_cols(slot, h)], send.at[i, h], recv_.at[i, h], {"kv": p}
        )

    def pass_on(dst, send, recv_, slot, h):
        ref = dst.at[:, head_cols(slot, h)]
        return rcopy(ref, ref, send.at[2, h], recv_.at[2, h], {"kv": sibling})

    def out_own(src, dst, i, h):
        return pltpu.make_async_copy(src.at[h], dst.at[:, head_cols(k, h)], loc_sem.at[i + h])

    def out_start(src, dst, send, recv_, i, h):
        out_copy(src, dst, send, recv_, 1, across, k, h).start()
        out_copy(src, dst, send, recv_, 0, sibling, k, h).start()
        out_own(src, dst, i, h).start()

    def out_forward(src, dst, send, recv_, i, h):
        out_copy(src, dst, send, recv_, 1, across, across, h).wait_recv()
        pass_on(dst, send, recv_, across, h).start()

    def out_finish(src, dst, send, recv_, i, h):
        out_own(src, dst, i, h).wait()
        out_copy(src, dst, send, recv_, 0, sibling, sibling, h).wait_recv()
        pass_on(dst, send, recv_, corner, h).wait_recv()
        for slot, p in ((0, sibling), (1, across)):
            out_copy(src, dst, send, recv_, slot, p, k, h).wait_send()
        pass_on(dst, send, recv_, across, h).wait_send()

    att_args = (att, att_out, att_s, att_r, 5)
    dq_args = (dq, dq_out, dq_s, dq_r, 7)

    def far_unit(u):
        h = jnp.where(u >= far, 1, 0)
        return z - (2 + u - h * far), h

    over_at = [jnp.minimum(done + 2, ends[0]), jnp.minimum(done + 3, ends[1])]

    def fwd_step(it):
        @pl.when(it < 2 * far)
        def _():
            o, h = far_unit(it)
            rcopy(ag.at[o, h, :, r], ag.at[o, h, :, r], zs.at[0, h], zr.at[o, h], dev_y).wait_recv()
            start(ag1(o, h))

        @pl.when((it >= LAG) & (it - LAG < 2 * far))
        def _():
            o, h = far_unit(it - LAG)
            recv(ag1_in(o, h))
            start(ag2(o, h))

        @pl.when((it >= 2 * LAG) & (it - 2 * LAG < 2 * far))
        def _():
            o, h = far_unit(it - 2 * LAG)
            recv(ag2_in(o, h))
            start(ag3(o, h))

        @pl.when(it < 4)
        def _():
            local = it % 2 == 1

            @pl.when(it == 1)
            def _():
                for c in own_kv:
                    c.wait()
                for p in peers:
                    recv(kv_copies(p, p))

            forward(
                jnp.where(local, nz, z),
                it // 2,
                jnp.where(local, 1, 0),
                jnp.where(local, 0, r * blk - 1),
                True,
            )

        def chunk(j, _):
            o, h = far_unit(it - 3 * LAG)
            inner = (j == 0) & (it >= 3 * LAG) & (it - 3 * LAG < 2 * far)
            second = jnp.where(j == 1, jnp.where(it == done + 1, 1, 0), jnp.where(it == over_at[1], 1, 0))
            below = (j == 1) & ((it == done) | (it == done + 1)) & has_down
            over = (j == 2) & ((it == over_at[0]) | (it == over_at[1])) & is_top & wrap

            @pl.when(inner)
            def _():
                recv(ag3_in(o, h))

            @pl.when(below)
            def _():
                up_copy(z - 1, second).wait_recv()

            if wrap:
                @pl.when(over)
                def _():
                    wrap_copy(0, second).wait_recv()

            @pl.when(inner | below | over)
            def _():
                forward(
                    jnp.where(j == 0, o, jnp.where(j == 1, z - 1, 0)), jnp.where(j == 0, h, second), 0, 0, False
                )

            return 0

        lax.fori_loop(0, 3, chunk, 0)

        @pl.when((it == ends[0]) | (it == ends[1]))
        def _():
            h = jnp.where(it == ends[1], 1, 0)
            total = jnp.sum(l[h], axis=1, keepdims=True)
            out = (acc[h] / total).astype(BF16)
            att[h] = out
            delta = jnp.sum(out.astype(F32) * do[h].astype(F32), axis=1, keepdims=True)
            lse_row[h] = jnp.transpose(m[h] + jnp.log2(total))[:8]
            delta_row[h] = jnp.transpose(jnp.broadcast_to(delta, (tok, HD)))[:8]
            out_start(*att_args, h)

    def backward(c, h, slope, offset, masked):
        tile_blocks = KEY_TILE // blk
        lse = lse_row[h, 0:1, :]
        delta = delta_row[h, 0:1, :]
        qh, doh = q[h], do[h]
        for t in range(plane_keys // KEY_TILE):
            bs = slice(t * tile_blocks, (t + 1) * tile_blocks)
            kk = ag[c, h, 0, bs].reshape(KEY_TILE, HD)
            vv = ag[c, h, 1, bs].reshape(KEY_TILE, HD)
            prob = jnp.exp2(dot(kk, qh, NT) * LOG2_SCALE - lse)
            if masked:
                row = lax.broadcasted_iota(jnp.int32, (1, tok), 1) * slope + offset
                key = lax.broadcasted_iota(jnp.int32, (KEY_TILE, tok), 0) + t * KEY_TILE
                prob = jnp.where(key <= row, prob, 0.0)
            ds = (prob * (dot(vv, doh, NT) - delta)).astype(BF16)
            grad[c, h, 1, bs] = dot(prob.astype(BF16), doh, NN).reshape(tile_blocks, blk, HD)
            grad[c, h, 0, bs] = (dot(ds, qh, NN) * SCALE).reshape(tile_blocks, blk, HD)
            dqt[h] += dot(kk, ds, TN)

    def rsc(o, h, i, src, dst, dev):
        return rcopy(src, dst, rs_s.at[o, h, i], rs_r.at[o, h, i], dev)

    def rs1(o, h):
        return [
            rsc(o, h, 0, s1.at[o, h, 0], r1.at[o, h, 0], dev_left),
            rsc(o, h, 1, s1.at[o, h, 1], r1.at[o, h, 1], dev_right),
        ]

    def rs2(o, h):
        return [
            rsc(o, h, 2, s2.at[o, h, 0], r2.at[o, h, 0], dev_left),
            rsc(o, h, 3, s2.at[o, h, 1], r2.at[o, h, 1], dev_right),
        ]

    def rs3(o, h):
        return [rsc(o, h, 4, s3.at[o, h], r3.at[o, h], dev_y)]

    def gz_copy(o, h):
        return rcopy(sz.at[o, h], rz.at[z, h], gz_s.at[o, h], gz_r.at[z, h], {"seq": o * PLANE + r})

    def down_copy(h):
        return rcopy(szl.at[0, h], rzl.at[0, h], gl_s.at[0, h], gl_r.at[0, h], dev_down)

    def around_copy(h):
        return rcopy(szl.at[1, h], rzl.at[1, h], gl_s.at[1, h], gl_r.at[1, h], dev_bottom)

    def two(xx):
        return pl.ds(xx * 2, 2)

    def reduce1(o, h):
        s1[o, h, 0] = grad[o, h, 0, two(opp)].astype(BF16)
        s1[o, h, 1] = grad[o, h, 1, two(opp)].astype(BF16)
        start(rs1(o, h))

    def reduce2(o, h):
        recv(rs1(o, h))
        s2[o, h, 0, 0] = (grad[o, h, 0, two(left)] + r1[o, h, 0].astype(F32)).astype(BF16)
        s2[o, h, 0, 1] = grad[o, h, 1, two(left)].astype(BF16)
        s2[o, h, 1, 0] = grad[o, h, 0, two(right)].astype(BF16)
        s2[o, h, 1, 1] = (grad[o, h, 1, two(right)] + r1[o, h, 1].astype(F32)).astype(BF16)
        start(rs2(o, h))

    def summed(o, h, t, yy):
        return grad[o, h, t, x * 2 + yy] + (r2[o, h, 0, t, yy].astype(F32) + r2[o, h, 1, t, yy].astype(F32))

    def reduce3(o, h):
        recv(rs2(o, h))
        for t in range(2):
            s3[o, h, t] = summed(o, h, t, yo).astype(BF16)
        start(rs3(o, h))

    def reduce4(o, h):
        recv(rs3(o, h))
        for t in range(2):
            sz[o, h, t] = (summed(o, h, t, y) + r3[o, h, t].astype(F32)).astype(BF16)
        gz_copy(o, h).start()

    def d0_copy(w, slot, h):
        return rcopy(s0.at[h, w], r0.at[h, slot], d0_s.at[h, w], d0_r.at[h, slot], {"seq": base + w})

    def fin_copy(h, t, p, slot):
        return rcopy(
            fin.at[h, t, :, part(p)],
            fin_in.at[t, :, :, head_cols(slot, h)],
            fin_s.at[h, t, p],
            fin_r.at[h, t, slot],
            {"kv": p},
        )

    def own_fin(h, t):
        return pltpu.make_async_copy(
            fin.at[h, t, :, part(k)], fin_in.at[t, :, :, head_cols(k, h)], loc_sem.at[9 + 2 * h + t]
        )

    def far_grad(g):
        h = jnp.where(g >= z, 1, 0)
        j = g - h * z
        return jnp.where(j == 0, z - 1, j - 1), h, j

    def in_plane(g):
        _, _, j = far_grad(g)
        whole = j == 0
        if wrap:
            whole = whole | ((j == 1) & is_top)
        return (g >= 0) & (g < 2 * z) & jnp.logical_not(whole)

    def bwd_step(g):
        o, h, j = far_grad(g)

        @pl.when(g < 2 * z)
        def _():
            backward(o, h, 0, 0, False)

            @pl.when(j == 0)
            def _():
                szl[0, h] = grad[z - 1, h].astype(BF16)
                down_copy(h).start()

            if wrap:
                @pl.when((j == 1) & is_top)
                def _():
                    szl[1, h] = grad[0, h].astype(BF16)
                    around_copy(h).start()

        @pl.when(in_plane(g))
        def _():
            reduce1(o, h)

        @pl.when((g >= 2 * z) & (g < 2 * z + 4))
        def _():
            n = g - 2 * z
            head, local = n // 2, n % 2 == 1
            backward(
                jnp.where(local, nz, z), head, jnp.where(local, 1, 0), jnp.where(local, 0, r * blk - 1), True
            )

            @pl.when(local)
            def _():
                dq[head] = jnp.transpose(dqt[head] * SCALE).astype(BF16)
                out_start(*dq_args, head)
                fin[head] = grad[nz, head].astype(BF16)
                for t in range(2):
                    own_fin(head, t).start()
                    for p in peers:
                        fin_copy(head, t, p, k).start()

            @pl.when(jnp.logical_not(local))
            def _():
                @pl.when(has_up)
                def _():
                    down_copy(head).wait_recv()
                    grad[z, head] += rzl[0, head].astype(F32)

                if wrap:
                    @pl.when(is_bottom)
                    def _():
                        around_copy(head).wait_recv()
                        grad[z, head] += rzl[1, head].astype(F32)

                for w in range(PLANE):
                    for t in range(2):
                        s0[head, w, t] = grad[z, head, t, w].astype(BF16)
                for w in mates:
                    d0_copy(w, r, head).start()

        for back, stage in ((3, reduce4), (2, reduce3), (1, reduce2)):
            @pl.when(in_plane(g - back * LAG))
            def _(back=back, stage=stage):
                stage(*far_grad(g - back * LAG)[:2])

    last_it = bwd_at + 2 * z + 3 * LAG - 1

    def step(it, _):
        @pl.when(it <= ends[1])
        def _():
            fwd_step(it)

        @pl.when(it >= bwd_at)
        def _():
            bwd_step(it - bwd_at)

        for h in range(heads):
            @pl.when(it == ends[h] + 4)
            def _(h=h):
                out_forward(*att_args, h)

        @pl.when(it == last_it)
        def _():
            out_forward(*dq_args, 0)

        return 0

    lax.fori_loop(0, last_it + 1, step, 0)
    out_forward(*dq_args, 1)
    for h in range(heads):
        for w in mates:
            d0_copy(w, w, h).wait_recv()
        for t in range(2):
            own[h, t] = functools.reduce(jnp.add, [r0[h, w, t].astype(F32) for w in mates], grad[z, h, t, r])

    def add_plane(o, _):
        for h in range(heads):
            rcopy(sz.at[0, h], rz.at[o, h], gz_s.at[0, h], gz_r.at[o, h], dev_y).wait_recv()
        own[...] += rz[o].astype(F32)
        return 0

    lax.fori_loop(z + 2, jnp.where(is_bottom, nz - 1, nz), add_plane, 0)
    tail[...] = own[...].astype(BF16)

    def tail_copy(p, slot):
        return rcopy(
            tail.at[:, :, part(p)],
            tail_in.at[pl.ds(slot * heads, heads)],
            tail_s.at[p],
            tail_r.at[slot],
            {"kv": p},
        )

    for p in peers:
        tail_copy(p, k).start()
    own_tail = pltpu.make_async_copy(
        tail.at[:, :, part(k)], tail_in.at[pl.ds(k * heads, heads)], loc_sem.at[13]
    )
    own_tail.start()
    for p in peers:
        sum_copy(p, k).wait_send()
        sent(kv_copies(p, k))
    for w in mates:
        first_copy(w, r).wait_send()

    def sent_head(h, _):
        for dz in range(2, nz - 1):
            @pl.when(z + dz < nz)
            def _(dz=dz):
                z_copy(dz, h).wait_send()

        @pl.when(has_up)
        def _():
            up_copy(z, h).wait_send()

        @pl.when(has_down)
        def _():
            down_copy(h).wait_send()

        if wrap:
            @pl.when(is_bottom)
            def _():
                wrap_copy(z, h).wait_send()

            @pl.when(is_top)
            def _():
                around_copy(h).wait_send()

        def sent_plane(o, _):
            direct = (o + 1 != z) & jnp.logical_not((o == 0) & is_top)

            @pl.when(direct)
            def _():
                sent(ag1(o, h) + ag2(o, h) + ag3(o, h) + rs1(o, h) + rs2(o, h) + rs3(o, h))
                gz_copy(o, h).wait_send()

            return 0

        for w in mates:
            d0_copy(w, r, h).wait_send()
        lax.fori_loop(0, z, sent_plane, 0)
        return 0

    lax.fori_loop(0, heads, sent_head, 0)
    for h in range(heads):
        out_finish(*att_args, h)
        out_finish(*dq_args, h)
    for h in range(heads):
        for t in range(2):
            own_fin(h, t).wait()
            for p in peers:
                fin_copy(h, t, p, p).wait_recv()
    own_tail.wait()
    for p in peers:
        tail_copy(p, p).wait_recv()
    results = [
        pltpu.make_async_copy(res.at[t], ref, loc_sem.at[14 + t]) for t, ref in enumerate((dk_out, dv_out))
    ]
    for t in range(2):
        arrived = jnp.concatenate([tail_in[h, t].astype(F32) for h in range(n_kv * heads)], axis=1)
        for b in range(blocks):
            res[t, b] = (fin_in[t, b].astype(F32) + jnp.where(summary == b, arrived, 0.0)).astype(BF16)
        results[t].start()

    for p in peers:
        tail_copy(p, k).wait_send()
        for h in range(heads):
            for t in range(2):
                fin_copy(h, t, p, k).wait_send()
    for c in results:
        c.wait()


def hand_over(*refs):
    n = (len(refs) - 2) // 3
    ins, outs, held = refs[:n], refs[n : 2 * n], refs[2 * n : 3 * n]
    load_sem, save_sem = refs[3 * n :]
    loads = [pltpu.make_async_copy(a, b, load_sem.at[i]) for i, (a, b) in enumerate(zip(ins, held))]
    saves = [pltpu.make_async_copy(a, b, save_sem.at[i]) for i, (a, b) in enumerate(zip(held, outs))]
    for c in loads:
        c.start()
    for load, save in zip(loads, saves):
        load.wait()
        save.start()
    for c in saves:
        c.wait()


def shards(queries, keys, values, layout, grad_out):
    tok, feat = queries.shape
    blocks, part_tok = keys.shape[0], keys.shape[1]
    n_kv = lax.axis_size("kv")
    nz = lax.axis_size("seq") // PLANE
    blk = part_tok * n_kv
    width = feat // n_kv
    heads = width // HD
    dma = pltpu.SemaphoreType.DMA

    def vm(*shape, dtype=BF16):
        return pltpu.VMEM(shape, dtype)

    results = tuple(jax.ShapeDtypeStruct(a.shape, BF16) for a in (queries, queries, keys, keys))
    hbm = [pl.BlockSpec(memory_space=pltpu.HBM)]
    made = pl.pallas_call(
        functools.partial(kernel, nz),
        out_shape=results,
        in_specs=hbm * 5,
        out_specs=hbm * 4,
        scratch_shapes=[
            vm(layout.shape[1], min(128, layout.shape[0]), dtype=jnp.int32),
            vm(*keys.shape),
            vm(*keys.shape),
            vm(heads, tok, HD),
            vm(heads, tok, HD),
            vm(n_kv * heads, 2, part_tok, HD),
            vm(nz + 1, heads, 2, PLANE, blk, HD),
            vm(nz + 1, heads, 2, PLANE, blk, HD, dtype=F32),
            vm(heads, tok, HD, dtype=F32),
            vm(heads, tok, HD, dtype=F32),
            vm(heads, tok, HD, dtype=F32),
            vm(heads, 8, tok, dtype=F32),
            vm(heads, 8, tok, dtype=F32),
            vm(heads, HD, tok, dtype=F32),
            vm(heads, tok, HD),
            vm(heads, tok, HD),
            vm(heads, 2, blocks, blk, HD),
            vm(2, blocks, part_tok, feat),
            vm(heads, 2, blk, HD),
            vm(n_kv * heads, 2, part_tok, HD),
            vm(2, blocks, part_tok, feat),
            vm(heads, PLANE, 2, blk, HD),
            vm(nz, heads, 2, 2, blk, HD),
            vm(nz, heads, 2, 2, 2, blk, HD),
            vm(nz, heads, 2, blk, HD),
            vm(nz, heads, 2, blk, HD),
            vm(2, heads, 2, PLANE, blk, HD),
            vm(heads, PLANE, 2, blk, HD),
            vm(nz, heads, 2, 2, blk, HD),
            vm(nz, heads, 2, 2, 2, blk, HD),
            vm(nz, heads, 2, blk, HD),
            vm(nz, heads, 2, blk, HD),
            vm(2, heads, 2, PLANE, blk, HD),
            vm(heads, 2, blk, HD, dtype=F32),
            dma((3 + 2 * heads,)),
            dma((n_kv,)),
            dma((n_kv,)),
            dma((heads, 2, n_kv)),
            dma((heads, 2, n_kv)),
            dma((nz, heads)),
            dma((nz, heads)),
            dma((2, heads)),
            dma((2, heads)),
            dma((nz, heads, 5)),
            dma((nz, heads, 5)),
            dma((nz, heads, 5)),
            dma((nz, heads, 5)),
            dma((nz, heads)),
            dma((nz, heads)),
            dma((2, heads)),
            dma((2, heads)),
            dma((3, heads)),
            dma((3, heads)),
            dma((3, heads)),
            dma((3, heads)),
            dma((heads, 2, n_kv)),
            dma((heads, 2, n_kv)),
            dma((n_kv,)),
            dma((n_kv,)),
            dma((PLANE,)),
            dma((PLANE,)),
            dma((heads, PLANE)),
            dma((heads, PLANE)),
            dma((16,)),
        ],
        compiler_params=pltpu.CompilerParams(
            collective_id=0, has_side_effects=True, vmem_limit_bytes=VMEM_LIMIT
        ),
    )(layout.T, queries, keys, values, grad_out)
    return pl.pallas_call(
        hand_over,
        out_shape=results,
        in_specs=hbm * 4,
        out_specs=hbm * 4,
        scratch_shapes=[*(vm(*a.shape) for a in results), dma((4,)), dma((4,))],
        compiler_params=pltpu.CompilerParams(vmem_limit_bytes=VMEM_LIMIT),
    )(*made)


def solution(mesh):
    return jax.shard_map(
        shards,
        mesh=mesh,
        in_specs=(P("seq", None), P("seq", "kv", None), P("seq", "kv", None), P(), P("seq", None)),
        out_specs=(P("seq", None), P("seq", None), P("seq", "kv", None), P("seq", "kv", None)),
        check_vma=False,
    )
```

```python
import functools
import math

import jax
import jax.numpy as jnp
from jax import lax
from jax.experimental import pallas as pl
from jax.experimental.pallas import tpu as pltpu
from jax.sharding import PartitionSpec as P

HD = 128
PLANE = 8
MESH = pl.DeviceIdType.MESH
F32 = jnp.float32
BF16 = jnp.bfloat16
SCALE = 1.0 / math.sqrt(HD)
LOG2_SCALE = math.log2(math.e) / math.sqrt(HD)
NT = (((1,), (1,)), ((), ()))
NN = (((1,), (0,)), ((), ()))
TN = (((0,), (0,)), ((), ()))
KEY_TILE = 256
LAG = 2
VMEM_LIMIT = 123 * 512 * 1024


def dot(a, b, dims):
    return lax.dot_general(a, b, dims, preferred_element_type=F32)


def kernel(
    nz, layout_hbm, q_hbm, k_hbm, v_hbm, do_hbm,
    att_out, dq_out, dk_out, dv_out,
    lay, k_in, v_in, q, do, sums, ag, grad, m, l, acc, lse_row, delta_row, dqt, att, dq, fin, fin_in, tail, tail_in, res,
    s0, s1, s2, s3, sz, szl, r0, r1, r2, r3, rz, rzl, own,
    load_sem, sum_s, sum_r, kv_s, kv_r, zs, zr, zl_s, zl_r, ag_s, ag_r, rs_s, rs_r, gz_s, gz_r,
    gl_s, gl_r, att_s, att_r, dq_s, dq_r, fin_s, fin_r, tail_s, tail_r, d0_s, d0_r, loc_sem,
):
    heads, tok, _ = q.shape
    width = heads * HD
    blocks, part_tok = k_in.shape[0], k_in.shape[1]
    blk = ag.shape[4]
    n_kv = lax.axis_size("kv")
    s = lax.axis_index("seq")
    k = lax.axis_index("kv")
    z, r = s // PLANE, s % PLANE
    x, y = r // 2, r % 2
    left, right, opp, yo = (x + 3) % 4, (x + 1) % 4, (x + 2) % 4, 1 - y
    base = z * PLANE
    dev_left = {"seq": base + left * 2 + y}
    dev_right = {"seq": base + right * 2 + y}
    dev_y = {"seq": base + x * 2 + yo}
    dev_up = {"seq": s + PLANE}
    dev_down = {"seq": s - PLANE}
    dev_top = {"seq": (nz - 1) * PLANE + r}
    dev_bottom = {"seq": r}
    has_up, has_down = z + 1 < nz, z > 0
    wrap = nz > 2
    is_bottom, is_top = z == 0, z == nz - 1
    peers = [(k + i) % n_kv for i in range(1, n_kv)]
    sibling = (k // 2) * 2 + (k + 1) % 2
    across = (k + 2) % n_kv
    corner = (sibling + 2) % n_kv
    far = jnp.maximum(0, jnp.minimum(z, nz - 2) - 2)
    done = 3 * LAG - 1
    ends = [far + done, jnp.maximum(2 * far + done, far + done + 1)]
    bwd_at = ends[0] + 1

    def peer_cols(p):
        return pl.ds(pl.multiple_of(p * width, width), width)

    cols = peer_cols(k)

    def head_cols(p, h):
        return pl.ds(pl.multiple_of(p * width + h * HD, HD), HD)

    def part(p):
        return pl.ds(pl.multiple_of(p * part_tok, part_tok), part_tok)

    def rcopy(src, dst, send, recv, dev):
        return pltpu.make_async_remote_copy(
            src_ref=src, dst_ref=dst, send_sem=send, recv_sem=recv, device_id=dev, device_id_type=MESH
        )

    barrier = pltpu.get_barrier_semaphore()
    mates = [(r + i) % PLANE for i in range(1, PLANE)]
    around = [(w, p) for w in [r] + mates for p in [k] + peers][1:]
    for w, p in around:
        pl.semaphore_signal(barrier, inc=1, device_id={"seq": base + w, "kv": p}, device_id_type=MESH)
    for i in range(1, nz):
        pl.semaphore_signal(
            barrier, inc=1, device_id={"seq": ((z + i) % nz) * PLANE + r}, device_id_type=MESH
        )
    loads = [
        pltpu.make_async_copy(src, dst, load_sem.at[i])
        for i, (src, dst) in enumerate(
            (
                (layout_hbm.at[:, pl.ds(layout_hbm.shape[1] - lay.shape[1], lay.shape[1])], lay),
                (k_hbm, k_in),
                (v_hbm, v_in),
                *((q_hbm.at[:, head_cols(k, h)], q.at[h]) for h in range(heads)),
                *((do_hbm.at[:, head_cols(k, h)], do.at[h]) for h in range(heads)),
            )
        )
    ]
    for c in loads:
        c.start()
    for c in loads[:3]:
        c.wait()
    entry = lax.broadcasted_iota(jnp.int32, (lay.shape[0], 1), 0)
    last_row = lay[:, lay.shape[1] - 1 :]
    named = jnp.where(entry == jnp.minimum(s, nz * PLANE - 2), last_row, 0)
    summary = jnp.clip(jnp.sum(named, axis=0, keepdims=True) - s * blocks, 0, blocks - 1)
    for t, ref in enumerate((k_in, v_in)):
        picked = ref[0]
        for b in range(1, blocks):
            picked = jnp.where(summary == b, ref[b], picked)
        for h in range(n_kv * heads):
            sums[h, t] = picked[:, h * HD : h * HD + HD]
    pl.semaphore_wait(barrier, len(around) + nz - 1)

    def sum_copy(w, p, from_w, slot):
        return rcopy(
            sums.at[pl.ds(p * heads, heads)],
            ag.at[z, :, :, from_w, part(slot)],
            sum_s.at[w, p],
            sum_r.at[from_w, slot],
            {"seq": base + w, "kv": p},
        )

    for w, p in around:
        sum_copy(w, p, r, k).start()
    own_sum = pltpu.make_async_copy(
        sums.at[pl.ds(k * heads, heads)], ag.at[z, :, :, r, part(k)], loc_sem.at[0]
    )
    own_sum.start()

    def kv_copies(p, slot):
        return [
            rcopy(
                ref.at[:, :, head_cols(p, h)],
                ag.at[nz, h, t, :, part(slot)],
                kv_s.at[h, t, p],
                kv_r.at[h, t, slot],
                {"kv": p},
            )
            for h in range(heads)
            for t, ref in enumerate((k_in, v_in))
        ]

    own_kv = [
        pltpu.make_async_copy(
            ref.at[:, :, head_cols(k, h)], ag.at[nz, h, t, :, part(k)], loc_sem.at[1 + 2 * h + t]
        )
        for h in range(heads)
        for t, ref in enumerate((k_in, v_in))
    ]
    for c in own_kv:
        c.start()
    own_sum.wait()
    for p in peers:
        sum_copy(r, p, r, p).wait_recv()


    def agc(o, h, i, ref, dev):
        return rcopy(ref, ref, ag_s.at[o, h, i], ag_r.at[o, h, i], dev)

    def block(o, h, xx, yy):
        return ag.at[o, h, :, xx * 2 + yy]

    def pair(o, h, xx):
        return ag.at[o, h, :, pl.ds(xx * 2, 2)]

    def pair_of(o, h, t, xx):
        return ag.at[o, h, t, pl.ds(xx * 2, 2)]

    def ag1(o, h):
        return [agc(o, h, 0, block(o, h, x, y), dev_y)]

    def ag1_in(o, h):
        return [agc(o, h, 0, block(o, h, x, yo), dev_y)]

    def ag2(o, h):
        return [agc(o, h, 1, pair(o, h, x), dev_right), agc(o, h, 2, pair(o, h, x), dev_left)]

    def ag2_in(o, h):
        return [agc(o, h, 1, pair(o, h, left), dev_left), agc(o, h, 2, pair(o, h, right), dev_right)]

    def ag3(o, h):
        return [
            agc(o, h, 3, pair_of(o, h, 0, left), dev_right),
            agc(o, h, 4, pair_of(o, h, 1, right), dev_left),
        ]

    def ag3_in(o, h):
        return [
            agc(o, h, 3, pair_of(o, h, 0, opp), dev_left),
            agc(o, h, 4, pair_of(o, h, 1, opp), dev_right),
        ]

    def start(copies):
        for c in copies:
            c.start()

    def recv(copies):
        for c in copies:
            c.wait_recv()

    def sent(copies):
        for c in copies:
            c.wait_send()

    def z_copy(dz, h):
        return rcopy(ag.at[z, h, :, r], ag.at[z, h, :, r], zs.at[dz, h], zr.at[z, h], {"seq": s + dz * PLANE})

    def up_copy(o, h):
        return rcopy(ag.at[o, h], ag.at[o, h], zl_s.at[0, h], zl_r.at[0, h], dev_up)

    def up2_copy(o, h):
        return rcopy(ag.at[o, h], ag.at[o, h], zl_s.at[2, h], zl_r.at[2, h], dev_up)

    def wrap_copy(o, h):
        return rcopy(ag.at[o, h], ag.at[o, h], zl_s.at[1, h], zl_r.at[1, h], dev_top)

    for h in range(heads):
        for dz in range(3, nz - 1):
            @pl.when(z + dz < nz)
            def _(dz=dz, h=h):
                z_copy(dz, h).start()

    for p in peers:
        start(kv_copies(p, k))
    m[...] = jnp.full_like(m, -1e30)
    l[...] = jnp.zeros_like(l)
    acc[...] = jnp.zeros_like(acc)
    dqt[...] = jnp.zeros_like(dqt)
    for c in loads[3:]:
        c.wait()
    for w, p in around[n_kv - 1 :]:
        sum_copy(w, p, w, p).wait_recv()
    for h in range(heads):
        @pl.when(has_up)
        def _(h=h):
            up_copy(z, h).start()

        if wrap:
            @pl.when(is_bottom)
            def _(h=h):
                wrap_copy(z, h).start()

    plane_keys = PLANE * blk

    def forward(c, h, slope, offset, masked):
        kk = ag[c, h, 0].reshape(plane_keys, HD)
        vv = ag[c, h, 1].reshape(plane_keys, HD)
        score = dot(q[h], kk, NT) * LOG2_SCALE
        tiles = [score[:, j * HD : j * HD + HD] for j in range(plane_keys // HD)]
        if masked:
            row = lax.broadcasted_iota(jnp.int32, (tok, 1), 0) * slope + offset
            lane = lax.broadcasted_iota(jnp.int32, (tok, HD), 1)
            tiles = [jnp.where(lane + j * HD <= row, t, -jnp.inf) for j, t in enumerate(tiles)]
        top = functools.reduce(jnp.maximum, tiles)
        m_old = m[h]
        m_new = jnp.maximum(m_old, jnp.max(top, axis=1, keepdims=True))
        alpha = jnp.exp2(m_old - m_new)
        weights = [jnp.exp2(t - m_new) for t in tiles]
        l[h] = l[h] * alpha + functools.reduce(jnp.add, weights)
        w = jnp.concatenate([t.astype(BF16) for t in weights], axis=1)
        acc[h] = acc[h] * alpha + dot(w, vv, NN)
        m[h] = m_new

    def out_copy(src, dst, send, recv_, i, p, slot, h):
        return rcopy(
            src.at[h], dst.at[:, head_cols(slot, h)], send.at[i, h], recv_.at[i, h], {"kv": p}
        )

    def pass_on(dst, send, recv_, slot, h):
        ref = dst.at[:, head_cols(slot, h)]
        return rcopy(ref, ref, send.at[2, h], recv_.at[2, h], {"kv": sibling})

    def out_own(src, dst, i, h):
        return pltpu.make_async_copy(src.at[h], dst.at[:, head_cols(k, h)], loc_sem.at[i + h])

    def out_start(src, dst, send, recv_, i, h):
        out_copy(src, dst, send, recv_, 1, across, k, h).start()
        out_copy(src, dst, send, recv_, 0, sibling, k, h).start()
        out_own(src, dst, i, h).start()

    def out_forward(src, dst, send, recv_, i, h):
        out_copy(src, dst, send, recv_, 1, across, across, h).wait_recv()
        pass_on(dst, send, recv_, across, h).start()

    def out_finish(src, dst, send, recv_, i, h):
        out_own(src, dst, i, h).wait()
        out_copy(src, dst, send, recv_, 0, sibling, sibling, h).wait_recv()
        pass_on(dst, send, recv_, corner, h).wait_recv()
        for slot, p in ((0, sibling), (1, across)):
            out_copy(src, dst, send, recv_, slot, p, k, h).wait_send()
        pass_on(dst, send, recv_, across, h).wait_send()

    att_args = (att, att_out, att_s, att_r, 5)
    dq_args = (dq, dq_out, dq_s, dq_r, 7)

    def far_unit(u):
        h = jnp.where(u >= far, 1, 0)
        return z - (3 + u - h * far), h

    over_at = [jnp.minimum(done + 2, ends[0]), jnp.minimum(done + 3, ends[1])]

    def fwd_step(it):
        @pl.when(it < 2 * far)
        def _():
            o, h = far_unit(it)
            rcopy(ag.at[o, h, :, r], ag.at[o, h, :, r], zs.at[0, h], zr.at[o, h], dev_y).wait_recv()
            start(ag1(o, h))

        @pl.when((it >= LAG) & (it - LAG < 2 * far))
        def _():
            o, h = far_unit(it - LAG)
            recv(ag1_in(o, h))
            start(ag2(o, h))

        @pl.when((it >= 2 * LAG) & (it - 2 * LAG < 2 * far))
        def _():
            o, h = far_unit(it - 2 * LAG)
            recv(ag2_in(o, h))
            start(ag3(o, h))

        @pl.when(it < 4)
        def _():
            local = it % 2 == 1

            @pl.when(it == 1)
            def _():
                for c in own_kv:
                    c.wait()
                for p in peers:
                    recv(kv_copies(p, p))

            forward(
                jnp.where(local, nz, z),
                it // 2,
                jnp.where(local, 1, 0),
                jnp.where(local, 0, r * blk - 1),
                True,
            )

        @pl.when(((it == done - 1) | (it == done)) & has_down)
        def _():
            h = it - (done - 1)
            up_copy(z - 1, h).wait_recv()

            @pl.when(has_up)
            def _():
                up2_copy(z - 1, h).start()

        def chunk(j, _):
            o, h = far_unit(it - 3 * LAG)
            inner = (j == 0) & (it >= 3 * LAG) & (it - 3 * LAG < 2 * far)
            later = jnp.where(j == 1, done + 1, jnp.where(j == 2, over_at[1], ends[1]))
            second = jnp.where(it == later, 1, 0)
            second_below = (j == 3) & ((it == ends[0]) | (it == ends[1])) & (z >= 2)
            below = (j == 1) & ((it == done) | (it == done + 1)) & has_down
            over = (j == 2) & ((it == over_at[0]) | (it == over_at[1])) & is_top & wrap

            @pl.when(inner)
            def _():
                recv(ag3_in(o, h))

            @pl.when(second_below)
            def _():
                up2_copy(z - 2, second).wait_recv()

            if wrap:
                @pl.when(over)
                def _():
                    wrap_copy(0, second).wait_recv()

            @pl.when(inner | below | over | second_below)
            def _():
                forward(
                    jnp.where(j == 0, o, jnp.where(j == 1, z - 1, jnp.where(j == 2, 0, z - 2))), jnp.where(j == 0, h, second), 0, 0, False
                )

            return 0

        lax.fori_loop(0, 4, chunk, 0)

        @pl.when((it == ends[0]) | (it == ends[1]))
        def _():
            h = jnp.where(it == ends[1], 1, 0)
            total = jnp.sum(l[h], axis=1, keepdims=True)
            out = (acc[h] / total).astype(BF16)
            att[h] = out
            delta = jnp.sum(out.astype(F32) * do[h].astype(F32), axis=1, keepdims=True)
            lse_row[h] = jnp.transpose(m[h] + jnp.log2(total))[:8]
            delta_row[h] = jnp.transpose(jnp.broadcast_to(delta, (tok, HD)))[:8]
            out_start(*att_args, h)

    def backward(c, h, slope, offset, masked):
        tile_blocks = KEY_TILE // blk
        lse = lse_row[h, 0:1, :]
        delta = delta_row[h, 0:1, :]
        qh, doh = q[h], do[h]
        for t in range(plane_keys // KEY_TILE):
            bs = slice(t * tile_blocks, (t + 1) * tile_blocks)
            kk = ag[c, h, 0, bs].reshape(KEY_TILE, HD)
            vv = ag[c, h, 1, bs].reshape(KEY_TILE, HD)
            prob = jnp.exp2(dot(kk, qh, NT) * LOG2_SCALE - lse)
            if masked:
                row = lax.broadcasted_iota(jnp.int32, (1, tok), 1) * slope + offset
                key = lax.broadcasted_iota(jnp.int32, (KEY_TILE, tok), 0) + t * KEY_TILE
                prob = jnp.where(key <= row, prob, 0.0)
            ds = (prob * (dot(vv, doh, NT) - delta)).astype(BF16)
            grad[c, h, 1, bs] = dot(prob.astype(BF16), doh, NN).reshape(tile_blocks, blk, HD)
            grad[c, h, 0, bs] = (dot(ds, qh, NN) * SCALE).reshape(tile_blocks, blk, HD)
            dqt[h] += dot(kk, ds, TN)

    def rsc(o, h, i, src, dst, dev):
        return rcopy(src, dst, rs_s.at[o, h, i], rs_r.at[o, h, i], dev)

    def rs1(o, h):
        return [
            rsc(o, h, 0, s1.at[o, h, 0], r1.at[o, h, 0], dev_left),
            rsc(o, h, 1, s1.at[o, h, 1], r1.at[o, h, 1], dev_right),
        ]

    def rs2(o, h):
        return [
            rsc(o, h, 2, s2.at[o, h, 0], r2.at[o, h, 0], dev_left),
            rsc(o, h, 3, s2.at[o, h, 1], r2.at[o, h, 1], dev_right),
        ]

    def rs3(o, h):
        return [rsc(o, h, 4, s3.at[o, h], r3.at[o, h], dev_y)]

    def gz_copy(o, h):
        return rcopy(sz.at[o, h], rz.at[z, h], gz_s.at[o, h], gz_r.at[z, h], {"seq": o * PLANE + r})

    def down_copy(h):
        return rcopy(szl.at[0, h], rzl.at[0, h], gl_s.at[0, h], gl_r.at[0, h], dev_down)

    def down2_copy(h):
        return rcopy(szl.at[2, h], rzl.at[2, h], gl_s.at[2, h], gl_r.at[2, h], dev_down)

    def around_copy(h):
        return rcopy(szl.at[1, h], rzl.at[1, h], gl_s.at[1, h], gl_r.at[1, h], dev_bottom)

    def two(xx):
        return pl.ds(xx * 2, 2)

    def reduce1(o, h):
        s1[o, h, 0] = grad[o, h, 0, two(opp)].astype(BF16)
        s1[o, h, 1] = grad[o, h, 1, two(opp)].astype(BF16)
        start(rs1(o, h))

    def reduce2(o, h):
        recv(rs1(o, h))
        s2[o, h, 0, 0] = (grad[o, h, 0, two(left)] + r1[o, h, 0].astype(F32)).astype(BF16)
        s2[o, h, 0, 1] = grad[o, h, 1, two(left)].astype(BF16)
        s2[o, h, 1, 0] = grad[o, h, 0, two(right)].astype(BF16)
        s2[o, h, 1, 1] = (grad[o, h, 1, two(right)] + r1[o, h, 1].astype(F32)).astype(BF16)
        start(rs2(o, h))

    def summed(o, h, t, yy):
        return grad[o, h, t, x * 2 + yy] + (r2[o, h, 0, t, yy].astype(F32) + r2[o, h, 1, t, yy].astype(F32))

    def reduce3(o, h):
        recv(rs2(o, h))
        for t in range(2):
            s3[o, h, t] = summed(o, h, t, yo).astype(BF16)
        start(rs3(o, h))

    def reduce4(o, h):
        recv(rs3(o, h))
        for t in range(2):
            sz[o, h, t] = (summed(o, h, t, y) + r3[o, h, t].astype(F32)).astype(BF16)
        gz_copy(o, h).start()

    def d0_copy(w, slot, h):
        return rcopy(s0.at[h, w], r0.at[h, slot], d0_s.at[h, w], d0_r.at[h, slot], {"seq": base + w})

    def fin_copy(h, t, p, slot):
        return rcopy(
            fin.at[h, t, :, part(p)],
            fin_in.at[t, :, :, head_cols(slot, h)],
            fin_s.at[h, t, p],
            fin_r.at[h, t, slot],
            {"kv": p},
        )

    def own_fin(h, t):
        return pltpu.make_async_copy(
            fin.at[h, t, :, part(k)], fin_in.at[t, :, :, head_cols(k, h)], loc_sem.at[9 + 2 * h + t]
        )

    def far_grad(g):
        h = jnp.where(g >= z, 1, 0)
        j = g - h * z
        next_at = jnp.minimum(z - 1, 4)
        furthest = j - 1 - jnp.where(j > next_at, 1, 0)
        return jnp.where(j == next_at, z - 1, jnp.where(j == 0, z - 2, furthest)), h

    def in_plane(g):
        o, _ = far_grad(g)
        return (g >= 0) & (g < 2 * z) & (z - o >= 3) & jnp.logical_not(is_top & (o == 0))

    def bwd_step(g):
        o, h = far_grad(g)

        @pl.when(g < 2 * z)
        def _():
            backward(o, h, 0, 0, False)

            @pl.when(o == z - 2)
            def _():
                szl[2, h] = grad[o, h].astype(BF16)
                down2_copy(h).start()

            @pl.when(o == z - 1)
            def _():
                @pl.when(has_up)
                def _():
                    down2_copy(h).wait_recv()
                    grad[z - 1, h] += rzl[2, h].astype(F32)

                szl[0, h] = grad[z - 1, h].astype(BF16)
                down_copy(h).start()

            @pl.when((o == 0) & is_top)
            def _():
                szl[1, h] = grad[0, h].astype(BF16)
                around_copy(h).start()

        @pl.when(in_plane(g))
        def _():
            reduce1(o, h)

        @pl.when((g >= 2 * z) & (g < 2 * z + 4))
        def _():
            n = g - 2 * z
            head, local = n // 2, n % 2 == 1
            backward(
                jnp.where(local, nz, z), head, jnp.where(local, 1, 0), jnp.where(local, 0, r * blk - 1), True
            )

            @pl.when(local)
            def _():
                dq[head] = jnp.transpose(dqt[head] * SCALE).astype(BF16)
                out_start(*dq_args, head)
                fin[head] = grad[nz, head].astype(BF16)
                for t in range(2):
                    own_fin(head, t).start()
                    for p in peers:
                        fin_copy(head, t, p, k).start()

            @pl.when(jnp.logical_not(local))
            def _():
                @pl.when(has_up)
                def _():
                    down_copy(head).wait_recv()
                    grad[z, head] += rzl[0, head].astype(F32)

                if wrap:
                    @pl.when(is_bottom)
                    def _():
                        around_copy(head).wait_recv()
                        grad[z, head] += rzl[1, head].astype(F32)

                for w in range(PLANE):
                    for t in range(2):
                        s0[head, w, t] = grad[z, head, t, w].astype(BF16)
                for w in mates:
                    d0_copy(w, r, head).start()

        for back, stage in ((3, reduce4), (2, reduce3), (1, reduce2)):
            @pl.when(in_plane(g - back * LAG))
            def _(back=back, stage=stage):
                stage(*far_grad(g - back * LAG))

    last_it = bwd_at + 2 * z + 3 * LAG - 1

    def step(it, _):
        @pl.when(it <= ends[1])
        def _():
            fwd_step(it)

        @pl.when(it >= bwd_at)
        def _():
            bwd_step(it - bwd_at)

        for h in range(heads):
            @pl.when(it == ends[h] + 4)
            def _(h=h):
                out_forward(*att_args, h)

        @pl.when(it == last_it)
        def _():
            out_forward(*dq_args, 0)

        return 0

    lax.fori_loop(0, last_it + 1, step, 0)
    out_forward(*dq_args, 1)
    for h in range(heads):
        for w in mates:
            d0_copy(w, w, h).wait_recv()
        for t in range(2):
            own[h, t] = functools.reduce(jnp.add, [r0[h, w, t].astype(F32) for w in mates], grad[z, h, t, r])

    def add_plane(o, _):
        for h in range(heads):
            rcopy(sz.at[0, h], rz.at[o, h], gz_s.at[0, h], gz_r.at[o, h], dev_y).wait_recv()
        own[...] += rz[o].astype(F32)
        return 0

    lax.fori_loop(z + 3, jnp.where(is_bottom, nz - 1, nz), add_plane, 0)
    tail[...] = own[...].astype(BF16)

    def tail_copy(p, slot):
        return rcopy(
            tail.at[:, :, part(p)],
            tail_in.at[pl.ds(slot * heads, heads)],
            tail_s.at[p],
            tail_r.at[slot],
            {"kv": p},
        )

    for p in peers:
        tail_copy(p, k).start()
    own_tail = pltpu.make_async_copy(
        tail.at[:, :, part(k)], tail_in.at[pl.ds(k * heads, heads)], loc_sem.at[13]
    )
    own_tail.start()
    for w, p in around:
        sum_copy(w, p, r, k).wait_send()
    for p in peers:
        sent(kv_copies(p, k))

    def sent_head(h, _):
        for dz in range(3, nz - 1):
            @pl.when(z + dz < nz)
            def _(dz=dz):
                z_copy(dz, h).wait_send()

        @pl.when(has_up)
        def _():
            up_copy(z, h).wait_send()

        @pl.when(has_up & has_down)
        def _():
            up2_copy(z - 1, h).wait_send()

        @pl.when(has_down)
        def _():
            down_copy(h).wait_send()

        @pl.when(z >= 2)
        def _():
            down2_copy(h).wait_send()

        if wrap:
            @pl.when(is_bottom)
            def _():
                wrap_copy(z, h).wait_send()

            @pl.when(is_top)
            def _():
                around_copy(h).wait_send()

        def sent_plane(o, _):
            direct = (z - o >= 3) & jnp.logical_not((o == 0) & is_top)

            @pl.when(direct)
            def _():
                sent(ag1(o, h) + ag2(o, h) + ag3(o, h) + rs1(o, h) + rs2(o, h) + rs3(o, h))
                gz_copy(o, h).wait_send()

            return 0

        for w in mates:
            d0_copy(w, r, h).wait_send()
        lax.fori_loop(0, z, sent_plane, 0)
        return 0

    lax.fori_loop(0, heads, sent_head, 0)
    for h in range(heads):
        out_finish(*att_args, h)
        out_finish(*dq_args, h)
    for h in range(heads):
        for t in range(2):
            own_fin(h, t).wait()
            for p in peers:
                fin_copy(h, t, p, p).wait_recv()
    own_tail.wait()
    for p in peers:
        tail_copy(p, p).wait_recv()
    results = [
        pltpu.make_async_copy(res.at[t], ref, loc_sem.at[14 + t]) for t, ref in enumerate((dk_out, dv_out))
    ]
    for t in range(2):
        arrived = jnp.concatenate([tail_in[h, t].astype(F32) for h in range(n_kv * heads)], axis=1)
        for b in range(blocks):
            res[t, b] = (fin_in[t, b].astype(F32) + jnp.where(summary == b, arrived, 0.0)).astype(BF16)
        results[t].start()

    for p in peers:
        tail_copy(p, k).wait_send()
        for h in range(heads):
            for t in range(2):
                fin_copy(h, t, p, k).wait_send()
    for c in results:
        c.wait()


def hand_over(*refs):
    n = (len(refs) - 2) // 3
    ins, outs, held = refs[:n], refs[n : 2 * n], refs[2 * n : 3 * n]
    load_sem, save_sem = refs[3 * n :]
    loads = [pltpu.make_async_copy(a, b, load_sem.at[i]) for i, (a, b) in enumerate(zip(ins, held))]
    saves = [pltpu.make_async_copy(a, b, save_sem.at[i]) for i, (a, b) in enumerate(zip(held, outs))]
    for c in loads:
        c.start()
    for load, save in zip(loads, saves):
        load.wait()
        save.start()
    for c in saves:
        c.wait()


def shards(queries, keys, values, layout, grad_out):
    tok, feat = queries.shape
    blocks, part_tok = keys.shape[0], keys.shape[1]
    n_kv = lax.axis_size("kv")
    nz = lax.axis_size("seq") // PLANE
    blk = part_tok * n_kv
    width = feat // n_kv
    heads = width // HD
    dma = pltpu.SemaphoreType.DMA

    def vm(*shape, dtype=BF16):
        return pltpu.VMEM(shape, dtype)

    results = tuple(jax.ShapeDtypeStruct(a.shape, BF16) for a in (queries, queries, keys, keys))
    hbm = [pl.BlockSpec(memory_space=pltpu.HBM)]
    made = pl.pallas_call(
        functools.partial(kernel, nz),
        out_shape=results,
        in_specs=hbm * 5,
        out_specs=hbm * 4,
        scratch_shapes=[
            vm(layout.shape[1], min(128, layout.shape[0]), dtype=jnp.int32),
            vm(*keys.shape),
            vm(*keys.shape),
            vm(heads, tok, HD),
            vm(heads, tok, HD),
            vm(n_kv * heads, 2, part_tok, HD),
            vm(nz + 1, heads, 2, PLANE, blk, HD),
            vm(nz + 1, heads, 2, PLANE, blk, HD, dtype=F32),
            vm(heads, tok, HD, dtype=F32),
            vm(heads, tok, HD, dtype=F32),
            vm(heads, tok, HD, dtype=F32),
            vm(heads, 8, tok, dtype=F32),
            vm(heads, 8, tok, dtype=F32),
            vm(heads, HD, tok, dtype=F32),
            vm(heads, tok, HD),
            vm(heads, tok, HD),
            vm(heads, 2, blocks, blk, HD),
            vm(2, blocks, part_tok, feat),
            vm(heads, 2, blk, HD),
            vm(n_kv * heads, 2, part_tok, HD),
            vm(2, blocks, part_tok, feat),
            vm(heads, PLANE, 2, blk, HD),
            vm(nz, heads, 2, 2, blk, HD),
            vm(nz, heads, 2, 2, 2, blk, HD),
            vm(nz, heads, 2, blk, HD),
            vm(nz, heads, 2, blk, HD),
            vm(3, heads, 2, PLANE, blk, HD),
            vm(heads, PLANE, 2, blk, HD),
            vm(nz, heads, 2, 2, blk, HD),
            vm(nz, heads, 2, 2, 2, blk, HD),
            vm(nz, heads, 2, blk, HD),
            vm(nz, heads, 2, blk, HD),
            vm(3, heads, 2, PLANE, blk, HD),
            vm(heads, 2, blk, HD, dtype=F32),
            dma((3 + 2 * heads,)),
            dma((PLANE, n_kv)),
            dma((PLANE, n_kv)),
            dma((heads, 2, n_kv)),
            dma((heads, 2, n_kv)),
            dma((nz, heads)),
            dma((nz, heads)),
            dma((3, heads)),
            dma((3, heads)),
            dma((nz, heads, 5)),
            dma((nz, heads, 5)),
            dma((nz, heads, 5)),
            dma((nz, heads, 5)),
            dma((nz, heads)),
            dma((nz, heads)),
            dma((3, heads)),
            dma((3, heads)),
            dma((3, heads)),
            dma((3, heads)),
            dma((3, heads)),
            dma((3, heads)),
            dma((heads, 2, n_kv)),
            dma((heads, 2, n_kv)),
            dma((n_kv,)),
            dma((n_kv,)),
            dma((heads, PLANE)),
            dma((heads, PLANE)),
            dma((16,)),
        ],
        compiler_params=pltpu.CompilerParams(
            collective_id=0, has_side_effects=True, vmem_limit_bytes=VMEM_LIMIT
        ),
    )(layout.T, queries, keys, values, grad_out)
    return pl.pallas_call(
        hand_over,
        out_shape=results,
        in_specs=hbm * 4,
        out_specs=hbm * 4,
        scratch_shapes=[*(vm(*a.shape) for a in results), dma((4,)), dma((4,))],
        compiler_params=pltpu.CompilerParams(vmem_limit_bytes=VMEM_LIMIT),
    )(*made)


def solution(mesh):
    return jax.shard_map(
        shards,
        mesh=mesh,
        in_specs=(P("seq", None), P("seq", "kv", None), P("seq", "kv", None), P(), P("seq", None)),
        out_specs=(P("seq", None), P("seq", None), P("seq", "kv", None), P("seq", "kv", None)),
        check_vma=False,
    )
```

```python
import functools
import math

import jax
import jax.numpy as jnp
from jax import lax
from jax.experimental import pallas as pl
from jax.experimental.pallas import tpu as pltpu
from jax.sharding import PartitionSpec as P

HD = 128
PLANE = 8
MESH = pl.DeviceIdType.MESH
F32 = jnp.float32
BF16 = jnp.bfloat16
SCALE = 1.0 / math.sqrt(HD)
LOG2_SCALE = math.log2(math.e) / math.sqrt(HD)
NT = (((1,), (1,)), ((), ()))
NN = (((1,), (0,)), ((), ()))
TN = (((0,), (0,)), ((), ()))
KEY_TILE = 256
LAG = 2
VMEM_LIMIT = 123 * 512 * 1024


def dot(a, b, dims):
    return lax.dot_general(a, b, dims, preferred_element_type=F32)


def kernel(
    nz, layout_hbm, q_hbm, k_hbm, v_hbm, do_hbm,
    att_out, dq_out, dk_out, dv_out,
    lay, k_in, v_in, q, do, sums, ag, grad, m, l, acc, lse_row, delta_row, dqt, att, dq, fin, fin_in, tail, tail_in, res,
    s0, s1, s2, s3, sz, szl, r0, r1, r2, r3, rz, rzl, own,
    load_sem, sum_s, sum_r, kv_s, kv_r, zs, zr, zl_s, zl_r, ag_s, ag_r, rs_s, rs_r, gz_s, gz_r,
    gl_s, gl_r, att_s, att_r, dq_s, dq_r, fin_s, fin_r, tail_s, tail_r, d0_s, d0_r, loc_sem,
):
    heads, tok, _ = q.shape
    width = heads * HD
    blocks, part_tok = k_in.shape[0], k_in.shape[1]
    blk = ag.shape[4]
    n_kv = lax.axis_size("kv")
    s = lax.axis_index("seq")
    k = lax.axis_index("kv")
    z, r = s // PLANE, s % PLANE
    x, y = r // 2, r % 2
    left, right, opp, yo = (x + 3) % 4, (x + 1) % 4, (x + 2) % 4, 1 - y
    base = z * PLANE
    dev_left = {"seq": base + left * 2 + y}
    dev_right = {"seq": base + right * 2 + y}
    dev_y = {"seq": base + x * 2 + yo}
    dev_up = {"seq": s + PLANE}
    dev_down = {"seq": s - PLANE}
    dev_top = {"seq": (nz - 1) * PLANE + r}
    dev_bottom = {"seq": r}
    has_up, has_down = z + 1 < nz, z > 0
    wrap = nz > 2
    is_bottom, is_top = z == 0, z == nz - 1
    peers = [(k + i) % n_kv for i in range(1, n_kv)]
    sibling = (k // 2) * 2 + (k + 1) % 2
    across = (k + 2) % n_kv
    corner = (sibling + 2) % n_kv
    far = jnp.maximum(0, jnp.minimum(z, nz - 2) - 2)
    done = 3 * LAG - 1
    ends = [far + done, jnp.maximum(2 * far + done, far + done + 1)]
    bwd_at = ends[0] + 1

    def peer_cols(p):
        return pl.ds(pl.multiple_of(p * width, width), width)

    cols = peer_cols(k)

    def head_cols(p, h):
        return pl.ds(pl.multiple_of(p * width + h * HD, HD), HD)

    def part(p):
        return pl.ds(pl.multiple_of(p * part_tok, part_tok), part_tok)

    def rcopy(src, dst, send, recv, dev):
        return pltpu.make_async_remote_copy(
            src_ref=src, dst_ref=dst, send_sem=send, recv_sem=recv, device_id=dev, device_id_type=MESH
        )

    barrier = pltpu.get_barrier_semaphore()
    mates = [(r + i) % PLANE for i in range(1, PLANE)]
    around = [(w, p) for w in [r] + mates for p in [k] + peers][1:]
    for w, p in around:
        pl.semaphore_signal(barrier, inc=1, device_id={"seq": base + w, "kv": p}, device_id_type=MESH)
    for i in range(1, nz):
        pl.semaphore_signal(
            barrier, inc=1, device_id={"seq": ((z + i) % nz) * PLANE + r}, device_id_type=MESH
        )
    loads = [
        pltpu.make_async_copy(src, dst, load_sem.at[i])
        for i, (src, dst) in enumerate(
            (
                (layout_hbm.at[:, pl.ds(layout_hbm.shape[1] - lay.shape[1], lay.shape[1])], lay),
                (k_hbm, k_in),
                (v_hbm, v_in),
                *((q_hbm.at[:, head_cols(k, h)], q.at[h]) for h in range(heads)),
                *((do_hbm.at[:, head_cols(k, h)], do.at[h]) for h in range(heads)),
            )
        )
    ]
    for c in loads:
        c.start()
    for c in loads[:3]:
        c.wait()
    entry = lax.broadcasted_iota(jnp.int32, (lay.shape[0], 1), 0)
    last_row = lay[:, lay.shape[1] - 1 :]
    named = jnp.where(entry == jnp.minimum(s, nz * PLANE - 2), last_row, 0)
    summary = jnp.clip(jnp.sum(named, axis=0, keepdims=True) - s * blocks, 0, blocks - 1)
    for t, ref in enumerate((k_in, v_in)):
        picked = ref[0]
        for b in range(1, blocks):
            picked = jnp.where(summary == b, ref[b], picked)
        for h in range(n_kv * heads):
            sums[h, t] = picked[:, h * HD : h * HD + HD]
    pl.semaphore_wait(barrier, len(around) + nz - 1)

    def sum_copy(w, p, from_w, slot):
        return rcopy(
            sums.at[pl.ds(p * heads, heads)],
            ag.at[z, :, :, from_w, part(slot)],
            sum_s.at[w, p],
            sum_r.at[from_w, slot],
            {"seq": base + w, "kv": p},
        )

    for w, p in around:
        sum_copy(w, p, r, k).start()
    own_sum = pltpu.make_async_copy(
        sums.at[pl.ds(k * heads, heads)], ag.at[z, :, :, r, part(k)], loc_sem.at[0]
    )
    own_sum.start()

    def kv_copies(p, slot):
        return [
            rcopy(
                ref.at[:, :, head_cols(p, h)],
                ag.at[nz, h, t, :, part(slot)],
                kv_s.at[h, t, p],
                kv_r.at[h, t, slot],
                {"kv": p},
            )
            for h in range(heads)
            for t, ref in enumerate((k_in, v_in))
        ]

    own_kv = [
        pltpu.make_async_copy(
            ref.at[:, :, head_cols(k, h)], ag.at[nz, h, t, :, part(k)], loc_sem.at[1 + 2 * h + t]
        )
        for h in range(heads)
        for t, ref in enumerate((k_in, v_in))
    ]
    for c in own_kv:
        c.start()
    own_sum.wait()
    for p in peers:
        sum_copy(r, p, r, p).wait_recv()


    def agc(o, h, i, ref, dev):
        return rcopy(ref, ref, ag_s.at[o, h, i], ag_r.at[o, h, i], dev)

    def block(o, h, xx, yy):
        return ag.at[o, h, :, xx * 2 + yy]

    def pair(o, h, xx):
        return ag.at[o, h, :, pl.ds(xx * 2, 2)]

    def pair_of(o, h, t, xx):
        return ag.at[o, h, t, pl.ds(xx * 2, 2)]

    def ag1(o, h):
        return [agc(o, h, 0, block(o, h, x, y), dev_y)]

    def ag1_in(o, h):
        return [agc(o, h, 0, block(o, h, x, yo), dev_y)]

    def ag2(o, h):
        return [agc(o, h, 1, pair(o, h, x), dev_right), agc(o, h, 2, pair(o, h, x), dev_left)]

    def ag2_in(o, h):
        return [agc(o, h, 1, pair(o, h, left), dev_left), agc(o, h, 2, pair(o, h, right), dev_right)]

    def ag3(o, h):
        return [
            agc(o, h, 3, pair_of(o, h, 0, left), dev_right),
            agc(o, h, 4, pair_of(o, h, 1, right), dev_left),
        ]

    def ag3_in(o, h):
        return [
            agc(o, h, 3, pair_of(o, h, 0, opp), dev_left),
            agc(o, h, 4, pair_of(o, h, 1, opp), dev_right),
        ]

    def start(copies):
        for c in copies:
            c.start()

    def recv(copies):
        for c in copies:
            c.wait_recv()

    def sent(copies):
        for c in copies:
            c.wait_send()

    def z_copy(dz, h):
        return rcopy(ag.at[z, h, :, r], ag.at[z, h, :, r], zs.at[dz, h], zr.at[z, h], {"seq": s + dz * PLANE})

    def up_copy(o, h):
        return rcopy(ag.at[o, h], ag.at[o, h], zl_s.at[0, h], zl_r.at[0, h], dev_up)

    def up2_copy(o, h):
        return rcopy(ag.at[o, h], ag.at[o, h], zl_s.at[2, h], zl_r.at[2, h], dev_up)

    def wrap_copy(o, h):
        return rcopy(ag.at[o, h], ag.at[o, h], zl_s.at[1, h], zl_r.at[1, h], dev_top)

    for h in range(heads):
        for dz in range(3, nz - 1):
            @pl.when(z + dz < nz)
            def _(dz=dz, h=h):
                z_copy(dz, h).start()

    for p in peers:
        start(kv_copies(p, k))
    m[...] = jnp.full_like(m, -1e30)
    l[...] = jnp.zeros_like(l)
    acc[...] = jnp.zeros_like(acc)
    dqt[...] = jnp.zeros_like(dqt)
    for c in loads[3:]:
        c.wait()
    for w, p in around[n_kv - 1 :]:
        sum_copy(w, p, w, p).wait_recv()
    for h in range(heads):
        @pl.when(has_up)
        def _(h=h):
            up_copy(z, h).start()

        if wrap:
            @pl.when(is_bottom)
            def _(h=h):
                wrap_copy(z, h).start()

    plane_keys = PLANE * blk

    def forward(c, h, slope, offset, masked):
        kk = ag[c, h, 0].reshape(plane_keys, HD)
        vv = ag[c, h, 1].reshape(plane_keys, HD)
        score = dot(q[h], kk, NT) * LOG2_SCALE
        tiles = [score[:, j * HD : j * HD + HD] for j in range(plane_keys // HD)]
        if masked:
            row = lax.broadcasted_iota(jnp.int32, (tok, 1), 0) * slope + offset
            lane = lax.broadcasted_iota(jnp.int32, (tok, HD), 1)
            tiles = [jnp.where(lane + j * HD <= row, t, -jnp.inf) for j, t in enumerate(tiles)]
        top = functools.reduce(jnp.maximum, tiles)
        m_old = m[h]
        m_new = jnp.maximum(m_old, jnp.max(top, axis=1, keepdims=True))
        alpha = jnp.exp2(m_old - m_new)
        weights = [jnp.exp2(t - m_new) for t in tiles]
        l[h] = l[h] * alpha + functools.reduce(jnp.add, weights)
        w = jnp.concatenate([t.astype(BF16) for t in weights], axis=1)
        acc[h] = acc[h] * alpha + dot(w, vv, NN)
        m[h] = m_new

    def out_copy(src, dst, send, recv_, i, p, slot, h):
        return rcopy(
            src.at[h], dst.at[:, head_cols(slot, h)], send.at[i, h], recv_.at[i, h], {"kv": p}
        )

    def pass_on(dst, send, recv_, slot, h):
        ref = dst.at[:, head_cols(slot, h)]
        return rcopy(ref, ref, send.at[2, h], recv_.at[2, h], {"kv": sibling})

    def out_own(src, dst, i, h):
        return pltpu.make_async_copy(src.at[h], dst.at[:, head_cols(k, h)], loc_sem.at[i + h])

    def out_start(src, dst, send, recv_, i, h):
        out_copy(src, dst, send, recv_, 1, across, k, h).start()
        out_copy(src, dst, send, recv_, 0, sibling, k, h).start()
        out_own(src, dst, i, h).start()

    def out_forward(src, dst, send, recv_, i, h):
        out_copy(src, dst, send, recv_, 1, across, across, h).wait_recv()
        pass_on(dst, send, recv_, across, h).start()

    def out_finish(src, dst, send, recv_, i, h):
        out_own(src, dst, i, h).wait()
        out_copy(src, dst, send, recv_, 0, sibling, sibling, h).wait_recv()
        pass_on(dst, send, recv_, corner, h).wait_recv()
        for slot, p in ((0, sibling), (1, across)):
            out_copy(src, dst, send, recv_, slot, p, k, h).wait_send()
        pass_on(dst, send, recv_, across, h).wait_send()

    att_args = (att, att_out, att_s, att_r, 5)
    dq_args = (dq, dq_out, dq_s, dq_r, 7)

    def far_unit(u):
        h = jnp.where(u >= far, 1, 0)
        return z - (3 + u - h * far), h

    over_at = [jnp.minimum(done + 2, ends[0]), jnp.minimum(done + 3, ends[1])]

    def fwd_step(it):
        @pl.when(it < 2 * far)
        def _():
            o, h = far_unit(it)
            rcopy(ag.at[o, h, :, r], ag.at[o, h, :, r], zs.at[0, h], zr.at[o, h], dev_y).wait_recv()
            start(ag1(o, h))

        @pl.when((it >= LAG) & (it - LAG < 2 * far))
        def _():
            o, h = far_unit(it - LAG)
            recv(ag1_in(o, h))
            start(ag2(o, h))

        @pl.when((it >= 2 * LAG) & (it - 2 * LAG < 2 * far))
        def _():
            o, h = far_unit(it - 2 * LAG)
            recv(ag2_in(o, h))
            start(ag3(o, h))

        @pl.when(it < 4)
        def _():
            local = it % 2 == 1

            @pl.when(it == 1)
            def _():
                for c in own_kv:
                    c.wait()
                for p in peers:
                    recv(kv_copies(p, p))

            forward(
                jnp.where(local, nz, z),
                it // 2,
                jnp.where(local, 1, 0),
                jnp.where(local, 0, r * blk - 1),
                True,
            )

        @pl.when(((it == done - 1) | (it == done)) & has_down)
        def _():
            h = it - (done - 1)
            up_copy(z - 1, h).wait_recv()

            @pl.when(has_up)
            def _():
                up2_copy(z - 1, h).start()

        def chunk(j, _):
            o, h = far_unit(it - 3 * LAG)
            inner = (j == 0) & (it >= 3 * LAG) & (it - 3 * LAG < 2 * far)
            later = jnp.where(j == 1, done + 1, jnp.where(j == 2, over_at[1], ends[1]))
            second = jnp.where(it == later, 1, 0)
            second_below = (j == 3) & ((it == ends[0]) | (it == ends[1])) & (z >= 2)
            below = (j == 1) & ((it == done) | (it == done + 1)) & has_down
            over = (j == 2) & ((it == over_at[0]) | (it == over_at[1])) & is_top & wrap

            @pl.when(inner)
            def _():
                recv(ag3_in(o, h))

            @pl.when(second_below)
            def _():
                up2_copy(z - 2, second).wait_recv()

            if wrap:
                @pl.when(over)
                def _():
                    wrap_copy(0, second).wait_recv()

            @pl.when(inner | below | over | second_below)
            def _():
                forward(
                    jnp.where(j == 0, o, jnp.where(j == 1, z - 1, jnp.where(j == 2, 0, z - 2))), jnp.where(j == 0, h, second), 0, 0, False
                )

            return 0

        lax.fori_loop(0, 4, chunk, 0)

        @pl.when((it == ends[0]) | (it == ends[1]))
        def _():
            h = jnp.where(it == ends[1], 1, 0)
            total = jnp.sum(l[h], axis=1, keepdims=True)
            out = (acc[h] / total).astype(BF16)
            att[h] = out
            delta = jnp.sum(out.astype(F32) * do[h].astype(F32), axis=1, keepdims=True)
            lse_row[h] = jnp.transpose(m[h] + jnp.log2(total))[:8]
            delta_row[h] = jnp.transpose(jnp.broadcast_to(delta, (tok, HD)))[:8]
            out_start(*att_args, h)

    def backward(c, h, slope, offset, masked):
        tile_blocks = KEY_TILE // blk
        lse = lse_row[h, 0:1, :]
        delta = delta_row[h, 0:1, :]
        qh, doh = q[h], do[h]
        for t in range(plane_keys // KEY_TILE):
            bs = slice(t * tile_blocks, (t + 1) * tile_blocks)
            kk = ag[c, h, 0, bs].reshape(KEY_TILE, HD)
            vv = ag[c, h, 1, bs].reshape(KEY_TILE, HD)
            prob = jnp.exp2(dot(kk, qh, NT) * LOG2_SCALE - lse)
            if masked:
                row = lax.broadcasted_iota(jnp.int32, (1, tok), 1) * slope + offset
                key = lax.broadcasted_iota(jnp.int32, (KEY_TILE, tok), 0) + t * KEY_TILE
                prob = jnp.where(key <= row, prob, 0.0)
            ds = (prob * (dot(vv, doh, NT) - delta)).astype(BF16)
            grad[c, h, 1, bs] = dot(prob.astype(BF16), doh, NN).reshape(tile_blocks, blk, HD)
            grad[c, h, 0, bs] = (dot(ds, qh, NN) * SCALE).reshape(tile_blocks, blk, HD)
            dqt[h] += dot(kk, ds, TN)

    def rsc(o, h, i, src, dst, dev):
        return rcopy(src, dst, rs_s.at[o, h, i], rs_r.at[o, h, i], dev)

    def rs1(o, h):
        return [
            rsc(o, h, 0, s1.at[o, h, 0], r1.at[o, h, 0], dev_left),
            rsc(o, h, 1, s1.at[o, h, 1], r1.at[o, h, 1], dev_right),
        ]

    def rs2(o, h):
        return [
            rsc(o, h, 2, s2.at[o, h, 0], r2.at[o, h, 0], dev_left),
            rsc(o, h, 3, s2.at[o, h, 1], r2.at[o, h, 1], dev_right),
        ]

    def rs3(o, h):
        return [rsc(o, h, 4, s3.at[o, h], r3.at[o, h], dev_y)]

    def gz_copy(o, h):
        return rcopy(sz.at[o, h], rz.at[z, h], gz_s.at[o, h], gz_r.at[z, h], {"seq": o * PLANE + r})

    def down_copy(h):
        return rcopy(szl.at[0, h], rzl.at[0, h], gl_s.at[0, h], gl_r.at[0, h], dev_down)

    def down2_copy(h):
        return rcopy(szl.at[2, h], rzl.at[2, h], gl_s.at[2, h], gl_r.at[2, h], dev_down)

    def around_copy(h):
        return rcopy(szl.at[1, h], rzl.at[1, h], gl_s.at[1, h], gl_r.at[1, h], dev_bottom)

    def two(xx):
        return pl.ds(xx * 2, 2)

    def reduce1(o, h):
        s1[o, h, 0] = grad[o, h, 0, two(opp)].astype(BF16)
        s1[o, h, 1] = grad[o, h, 1, two(opp)].astype(BF16)
        start(rs1(o, h))

    def reduce2(o, h):
        recv(rs1(o, h))
        s2[o, h, 0, 0] = (grad[o, h, 0, two(left)] + r1[o, h, 0].astype(F32)).astype(BF16)
        s2[o, h, 0, 1] = grad[o, h, 1, two(left)].astype(BF16)
        s2[o, h, 1, 0] = grad[o, h, 0, two(right)].astype(BF16)
        s2[o, h, 1, 1] = (grad[o, h, 1, two(right)] + r1[o, h, 1].astype(F32)).astype(BF16)
        start(rs2(o, h))

    def summed(o, h, t, yy):
        return grad[o, h, t, x * 2 + yy] + (r2[o, h, 0, t, yy].astype(F32) + r2[o, h, 1, t, yy].astype(F32))

    def reduce3(o, h):
        recv(rs2(o, h))
        for t in range(2):
            s3[o, h, t] = summed(o, h, t, yo).astype(BF16)
        start(rs3(o, h))

    def reduce4(o, h):
        recv(rs3(o, h))
        for t in range(2):
            sz[o, h, t] = (summed(o, h, t, y) + r3[o, h, t].astype(F32)).astype(BF16)
        gz_copy(o, h).start()

    def d0_copy(w, slot, h):
        return rcopy(s0.at[h, w], r0.at[h, slot], d0_s.at[h, w], d0_r.at[h, slot], {"seq": base + w})

    def fin_copy(h, t, p, slot):
        return rcopy(
            fin.at[h, t, :, part(p)],
            fin_in.at[t, :, :, head_cols(slot, h)],
            fin_s.at[h, t, p],
            fin_r.at[h, t, slot],
            {"kv": p},
        )

    def own_fin(h, t):
        return pltpu.make_async_copy(
            fin.at[h, t, :, part(k)], fin_in.at[t, :, :, head_cols(k, h)], loc_sem.at[9 + 2 * h + t]
        )

    def far_grad(g):
        h = jnp.where(g >= z, 1, 0)
        j = g - h * z
        next_at = jnp.minimum(z - 1, 5)
        furthest = j - 1 - jnp.where(j > next_at, 1, 0)
        furthest = jnp.where(is_top, jnp.where(furthest == z - 3, 0, furthest + 1), furthest)
        return jnp.where(j == next_at, z - 1, jnp.where(j == 0, z - 2, furthest)), h

    def in_plane(g):
        o, _ = far_grad(g)
        return (g >= 0) & (g < 2 * z) & (z - o >= 3) & jnp.logical_not(is_top & (o == 0))

    def bwd_step(g):
        o, h = far_grad(g)

        @pl.when(g < 2 * z)
        def _():
            backward(o, h, 0, 0, False)

            @pl.when(o == z - 2)
            def _():
                szl[2, h] = grad[o, h].astype(BF16)
                down2_copy(h).start()

            @pl.when(o == z - 1)
            def _():
                @pl.when(has_up)
                def _():
                    down2_copy(h).wait_recv()
                    grad[z - 1, h] += rzl[2, h].astype(F32)

                szl[0, h] = grad[z - 1, h].astype(BF16)
                down_copy(h).start()

            @pl.when((o == 0) & is_top)
            def _():
                szl[1, h] = grad[0, h].astype(BF16)
                around_copy(h).start()

        @pl.when(in_plane(g))
        def _():
            reduce1(o, h)

        @pl.when((g >= 2 * z) & (g < 2 * z + 4))
        def _():
            n = g - 2 * z
            head, local = n // 2, (n == 1) | (n == 2)
            backward(
                jnp.where(local, nz, z), head, jnp.where(local, 1, 0), jnp.where(local, 0, r * blk - 1), True
            )

            @pl.when(n % 2 == 1)
            def _():
                dq[head] = jnp.transpose(dqt[head] * SCALE).astype(BF16)
                out_start(*dq_args, head)

            @pl.when(local)
            def _():
                fin[head] = grad[nz, head].astype(BF16)
                for t in range(2):
                    own_fin(head, t).start()
                    for p in peers:
                        fin_copy(head, t, p, k).start()

            @pl.when(jnp.logical_not(local))
            def _():
                @pl.when(has_up)
                def _():
                    down_copy(head).wait_recv()
                    grad[z, head] += rzl[0, head].astype(F32)

                if wrap:
                    @pl.when(is_bottom)
                    def _():
                        around_copy(head).wait_recv()
                        grad[z, head] += rzl[1, head].astype(F32)

                for w in range(PLANE):
                    for t in range(2):
                        s0[head, w, t] = grad[z, head, t, w].astype(BF16)
                for w in mates:
                    d0_copy(w, r, head).start()

        for back, stage in ((3, reduce4), (2, reduce3), (1, reduce2)):
            @pl.when(in_plane(g - back * LAG))
            def _(back=back, stage=stage):
                stage(*far_grad(g - back * LAG))

    last_it = bwd_at + 2 * z + 3 * LAG - 1

    def step(it, _):
        @pl.when(it <= ends[1])
        def _():
            fwd_step(it)

        @pl.when(it >= bwd_at)
        def _():
            bwd_step(it - bwd_at)

        for h in range(heads):
            @pl.when(it == ends[h] + 4)
            def _(h=h):
                out_forward(*att_args, h)

        @pl.when(it == last_it)
        def _():
            out_forward(*dq_args, 0)

        return 0

    lax.fori_loop(0, last_it + 1, step, 0)
    out_forward(*dq_args, 1)
    for h in range(heads):
        for w in mates:
            d0_copy(w, w, h).wait_recv()
        for t in range(2):
            own[h, t] = functools.reduce(jnp.add, [r0[h, w, t].astype(F32) for w in mates], grad[z, h, t, r])

    def add_plane(o, _):
        for h in range(heads):
            rcopy(sz.at[0, h], rz.at[o, h], gz_s.at[0, h], gz_r.at[o, h], dev_y).wait_recv()
        own[...] += rz[o].astype(F32)
        return 0

    lax.fori_loop(z + 3, jnp.where(is_bottom, nz - 1, nz), add_plane, 0)
    tail[...] = own[...].astype(BF16)

    def tail_copy(p, slot):
        return rcopy(
            tail.at[:, :, part(p)],
            tail_in.at[pl.ds(slot * heads, heads)],
            tail_s.at[p],
            tail_r.at[slot],
            {"kv": p},
        )

    for p in peers:
        tail_copy(p, k).start()
    own_tail = pltpu.make_async_copy(
        tail.at[:, :, part(k)], tail_in.at[pl.ds(k * heads, heads)], loc_sem.at[13]
    )
    own_tail.start()
    for w, p in around:
        sum_copy(w, p, r, k).wait_send()
    for p in peers:
        sent(kv_copies(p, k))

    def sent_head(h, _):
        for dz in range(3, nz - 1):
            @pl.when(z + dz < nz)
            def _(dz=dz):
                z_copy(dz, h).wait_send()

        @pl.when(has_up)
        def _():
            up_copy(z, h).wait_send()

        @pl.when(has_up & has_down)
        def _():
            up2_copy(z - 1, h).wait_send()

        @pl.when(has_down)
        def _():
            down_copy(h).wait_send()

        @pl.when(z >= 2)
        def _():
            down2_copy(h).wait_send()

        if wrap:
            @pl.when(is_bottom)
            def _():
                wrap_copy(z, h).wait_send()

            @pl.when(is_top)
            def _():
                around_copy(h).wait_send()

        def sent_plane(o, _):
            direct = (z - o >= 3) & jnp.logical_not((o == 0) & is_top)

            @pl.when(direct)
            def _():
                sent(ag1(o, h) + ag2(o, h) + ag3(o, h) + rs1(o, h) + rs2(o, h) + rs3(o, h))
                gz_copy(o, h).wait_send()

            return 0

        for w in mates:
            d0_copy(w, r, h).wait_send()
        lax.fori_loop(0, z, sent_plane, 0)
        return 0

    lax.fori_loop(0, heads, sent_head, 0)
    for h in range(heads):
        out_finish(*att_args, h)
        out_finish(*dq_args, h)
    for h in range(heads):
        for t in range(2):
            own_fin(h, t).wait()
            for p in peers:
                fin_copy(h, t, p, p).wait_recv()
    own_tail.wait()
    for p in peers:
        tail_copy(p, p).wait_recv()
    results = [
        pltpu.make_async_copy(res.at[t], ref, loc_sem.at[14 + t]) for t, ref in enumerate((dk_out, dv_out))
    ]
    for t in range(2):
        arrived = jnp.concatenate([tail_in[h, t].astype(F32) for h in range(n_kv * heads)], axis=1)
        for b in range(blocks):
            res[t, b] = (fin_in[t, b].astype(F32) + jnp.where(summary == b, arrived, 0.0)).astype(BF16)
        results[t].start()

    for p in peers:
        tail_copy(p, k).wait_send()
        for h in range(heads):
            for t in range(2):
                fin_copy(h, t, p, k).wait_send()
    for c in results:
        c.wait()


def hand_over(*refs):
    n = (len(refs) - 2) // 3
    ins, outs, held = refs[:n], refs[n : 2 * n], refs[2 * n : 3 * n]
    load_sem, save_sem = refs[3 * n :]
    loads = [pltpu.make_async_copy(a, b, load_sem.at[i]) for i, (a, b) in enumerate(zip(ins, held))]
    saves = [pltpu.make_async_copy(a, b, save_sem.at[i]) for i, (a, b) in enumerate(zip(held, outs))]
    for c in loads:
        c.start()
    for load, save in zip(loads, saves):
        load.wait()
        save.start()
    for c in saves:
        c.wait()


def shards(queries, keys, values, layout, grad_out):
    tok, feat = queries.shape
    blocks, part_tok = keys.shape[0], keys.shape[1]
    n_kv = lax.axis_size("kv")
    nz = lax.axis_size("seq") // PLANE
    blk = part_tok * n_kv
    width = feat // n_kv
    heads = width // HD
    dma = pltpu.SemaphoreType.DMA

    def vm(*shape, dtype=BF16):
        return pltpu.VMEM(shape, dtype)

    results = tuple(jax.ShapeDtypeStruct(a.shape, BF16) for a in (queries, queries, keys, keys))
    hbm = [pl.BlockSpec(memory_space=pltpu.HBM)]
    made = pl.pallas_call(
        functools.partial(kernel, nz),
        out_shape=results,
        in_specs=hbm * 5,
        out_specs=hbm * 4,
        scratch_shapes=[
            vm(layout.shape[1], min(128, layout.shape[0]), dtype=jnp.int32),
            vm(*keys.shape),
            vm(*keys.shape),
            vm(heads, tok, HD),
            vm(heads, tok, HD),
            vm(n_kv * heads, 2, part_tok, HD),
            vm(nz + 1, heads, 2, PLANE, blk, HD),
            vm(nz + 1, heads, 2, PLANE, blk, HD, dtype=F32),
            vm(heads, tok, HD, dtype=F32),
            vm(heads, tok, HD, dtype=F32),
            vm(heads, tok, HD, dtype=F32),
            vm(heads, 8, tok, dtype=F32),
            vm(heads, 8, tok, dtype=F32),
            vm(heads, HD, tok, dtype=F32),
            vm(heads, tok, HD),
            vm(heads, tok, HD),
            vm(heads, 2, blocks, blk, HD),
            vm(2, blocks, part_tok, feat),
            vm(heads, 2, blk, HD),
            vm(n_kv * heads, 2, part_tok, HD),
            vm(2, blocks, part_tok, feat),
            vm(heads, PLANE, 2, blk, HD),
            vm(nz, heads, 2, 2, blk, HD),
            vm(nz, heads, 2, 2, 2, blk, HD),
            vm(nz, heads, 2, blk, HD),
            vm(nz, heads, 2, blk, HD),
            vm(3, heads, 2, PLANE, blk, HD),
            vm(heads, PLANE, 2, blk, HD),
            vm(nz, heads, 2, 2, blk, HD),
            vm(nz, heads, 2, 2, 2, blk, HD),
            vm(nz, heads, 2, blk, HD),
            vm(nz, heads, 2, blk, HD),
            vm(3, heads, 2, PLANE, blk, HD),
            vm(heads, 2, blk, HD, dtype=F32),
            dma((3 + 2 * heads,)),
            dma((PLANE, n_kv)),
            dma((PLANE, n_kv)),
            dma((heads, 2, n_kv)),
            dma((heads, 2, n_kv)),
            dma((nz, heads)),
            dma((nz, heads)),
            dma((3, heads)),
            dma((3, heads)),
            dma((nz, heads, 5)),
            dma((nz, heads, 5)),
            dma((nz, heads, 5)),
            dma((nz, heads, 5)),
            dma((nz, heads)),
            dma((nz, heads)),
            dma((3, heads)),
            dma((3, heads)),
            dma((3, heads)),
            dma((3, heads)),
            dma((3, heads)),
            dma((3, heads)),
            dma((heads, 2, n_kv)),
            dma((heads, 2, n_kv)),
            dma((n_kv,)),
            dma((n_kv,)),
            dma((heads, PLANE)),
            dma((heads, PLANE)),
            dma((16,)),
        ],
        compiler_params=pltpu.CompilerParams(
            collective_id=0, has_side_effects=True, vmem_limit_bytes=VMEM_LIMIT
        ),
    )(layout.T, queries, keys, values, grad_out)
    return pl.pallas_call(
        hand_over,
        out_shape=results,
        in_specs=hbm * 4,
        out_specs=hbm * 4,
        scratch_shapes=[*(vm(*a.shape) for a in results), dma((4,)), dma((4,))],
        compiler_params=pltpu.CompilerParams(vmem_limit_bytes=VMEM_LIMIT),
    )(*made)


def solution(mesh):
    return jax.shard_map(
        shards,
        mesh=mesh,
        in_specs=(P("seq", None), P("seq", "kv", None), P("seq", "kv", None), P(), P("seq", None)),
        out_specs=(P("seq", None), P("seq", None), P("seq", "kv", None), P("seq", "kv", None)),
        check_vma=False,
    )
```

```python
import functools
import math

import jax
import jax.numpy as jnp
from jax import lax
from jax.experimental import pallas as pl
from jax.experimental.pallas import tpu as pltpu
from jax.sharding import PartitionSpec as P

HD = 128
PLANE = 8
MESH = pl.DeviceIdType.MESH
F32 = jnp.float32
BF16 = jnp.bfloat16
SCALE = 1.0 / math.sqrt(HD)
LOG2_SCALE = math.log2(math.e) / math.sqrt(HD)
NT = (((1,), (1,)), ((), ()))
NN = (((1,), (0,)), ((), ()))
TN = (((0,), (0,)), ((), ()))
KEY_TILE = 256
LAG = 2
VMEM_LIMIT = 123 * 512 * 1024


def dot(a, b, dims):
    return lax.dot_general(a, b, dims, preferred_element_type=F32)


def kernel(
    nz, layout_hbm, q_hbm, k_hbm, v_hbm, do_hbm,
    att_out, dq_out, dk_out, dv_out,
    lay, k_in, v_in, q, do, sums, ag, grad, m, l, acc, lse_row, delta_row, dqt, att, dq, fin, fin_in, tail, tail_in, res,
    s0, s1, s2, s3, sz, szl, r0, r1, r2, r3, rz, rzl, own,
    load_sem, sum_s, sum_r, kv_s, kv_r, zs, zr, zl_s, zl_r, ag_s, ag_r, rs_s, rs_r, gz_s, gz_r,
    gl_s, gl_r, att_s, att_r, dq_s, dq_r, fin_s, fin_r, tail_s, tail_r, d0_s, d0_r, loc_sem,
):
    heads, tok, _ = q.shape
    width = heads * HD
    blocks, part_tok = k_in.shape[0], k_in.shape[1]
    blk = ag.shape[4]
    n_kv = lax.axis_size("kv")
    s = lax.axis_index("seq")
    k = lax.axis_index("kv")
    z, r = s // PLANE, s % PLANE
    x, y = r // 2, r % 2
    left, right, opp, yo = (x + 3) % 4, (x + 1) % 4, (x + 2) % 4, 1 - y
    base = z * PLANE
    dev_left = {"seq": base + left * 2 + y}
    dev_right = {"seq": base + right * 2 + y}
    dev_y = {"seq": base + x * 2 + yo}
    dev_up = {"seq": s + PLANE}
    dev_down = {"seq": s - PLANE}
    dev_top = {"seq": (nz - 1) * PLANE + r}
    dev_bottom = {"seq": r}
    has_up, has_down = z + 1 < nz, z > 0
    wrap = nz > 2
    is_bottom, is_top = z == 0, z == nz - 1
    peers = [(k + i) % n_kv for i in range(1, n_kv)]
    sibling = (k // 2) * 2 + (k + 1) % 2
    across = (k + 2) % n_kv
    corner = (sibling + 2) % n_kv
    far = jnp.maximum(0, jnp.minimum(z, nz - 2) - 2)
    done = 3 * LAG - 1
    ends = [far + done, jnp.maximum(2 * far + done, far + done + 1)]
    bwd_at = ends[0] + 1

    def peer_cols(p):
        return pl.ds(pl.multiple_of(p * width, width), width)

    cols = peer_cols(k)

    def head_cols(p, h):
        return pl.ds(pl.multiple_of(p * width + h * HD, HD), HD)

    def part(p):
        return pl.ds(pl.multiple_of(p * part_tok, part_tok), part_tok)

    def rcopy(src, dst, send, recv, dev):
        return pltpu.make_async_remote_copy(
            src_ref=src, dst_ref=dst, send_sem=send, recv_sem=recv, device_id=dev, device_id_type=MESH
        )

    barrier = pltpu.get_barrier_semaphore()
    mates = [(r + i) % PLANE for i in range(1, PLANE)]
    around = [(w, p) for w in [r] + mates for p in [k] + peers][1:]
    for w, p in around:
        pl.semaphore_signal(barrier, inc=1, device_id={"seq": base + w, "kv": p}, device_id_type=MESH)
    for i in range(1, nz):
        pl.semaphore_signal(
            barrier, inc=1, device_id={"seq": ((z + i) % nz) * PLANE + r}, device_id_type=MESH
        )
    loads = [
        pltpu.make_async_copy(src, dst, load_sem.at[i])
        for i, (src, dst) in enumerate(
            (
                (layout_hbm.at[:, pl.ds(layout_hbm.shape[1] - lay.shape[1], lay.shape[1])], lay),
                (k_hbm, k_in),
                (v_hbm, v_in),
                *((q_hbm.at[:, head_cols(k, h)], q.at[h]) for h in range(heads)),
                *((do_hbm.at[:, head_cols(k, h)], do.at[h]) for h in range(heads)),
            )
        )
    ]
    for c in loads:
        c.start()
    for c in loads[:3]:
        c.wait()
    entry = lax.broadcasted_iota(jnp.int32, (lay.shape[0], 1), 0)
    last_row = lay[:, lay.shape[1] - 1 :]
    named = jnp.where(entry == jnp.minimum(s, nz * PLANE - 2), last_row, 0)
    summary = jnp.clip(jnp.sum(named, axis=0, keepdims=True) - s * blocks, 0, blocks - 1)
    for t, ref in enumerate((k_in, v_in)):
        picked = ref[0]
        for b in range(1, blocks):
            picked = jnp.where(summary == b, ref[b], picked)
        for h in range(n_kv * heads):
            sums[h, t] = picked[:, h * HD : h * HD + HD]
    pl.semaphore_wait(barrier, len(around) + nz - 1)

    def sum_copy(w, p, from_w, slot):
        return rcopy(
            sums.at[pl.ds(p * heads, heads)],
            ag.at[z, :, :, from_w, part(slot)],
            sum_s.at[w, p],
            sum_r.at[from_w, slot],
            {"seq": base + w, "kv": p},
        )

    for w, p in around:
        sum_copy(w, p, r, k).start()
    own_sum = pltpu.make_async_copy(
        sums.at[pl.ds(k * heads, heads)], ag.at[z, :, :, r, part(k)], loc_sem.at[0]
    )
    own_sum.start()

    def kv_copies(p, slot):
        return [
            rcopy(
                ref.at[:, :, head_cols(p, h)],
                ag.at[nz, h, t, :, part(slot)],
                kv_s.at[h, t, p],
                kv_r.at[h, t, slot],
                {"kv": p},
            )
            for h in range(heads)
            for t, ref in enumerate((k_in, v_in))
        ]

    own_kv = [
        pltpu.make_async_copy(
            ref.at[:, :, head_cols(k, h)], ag.at[nz, h, t, :, part(k)], loc_sem.at[1 + 2 * h + t]
        )
        for h in range(heads)
        for t, ref in enumerate((k_in, v_in))
    ]
    for c in own_kv:
        c.start()
    own_sum.wait()
    for p in peers:
        sum_copy(r, p, r, p).wait_recv()


    def agc(o, h, i, ref, dev):
        return rcopy(ref, ref, ag_s.at[o, h, i], ag_r.at[o, h, i], dev)

    def block(o, h, xx, yy):
        return ag.at[o, h, :, xx * 2 + yy]

    def pair(o, h, xx):
        return ag.at[o, h, :, pl.ds(xx * 2, 2)]

    def pair_of(o, h, t, xx):
        return ag.at[o, h, t, pl.ds(xx * 2, 2)]

    def ag1(o, h):
        return [agc(o, h, 0, block(o, h, x, y), dev_y)]

    def ag1_in(o, h):
        return [agc(o, h, 0, block(o, h, x, yo), dev_y)]

    def ag2(o, h):
        return [agc(o, h, 1, pair(o, h, x), dev_right), agc(o, h, 2, pair(o, h, x), dev_left)]

    def ag2_in(o, h):
        return [agc(o, h, 1, pair(o, h, left), dev_left), agc(o, h, 2, pair(o, h, right), dev_right)]

    def ag3(o, h):
        return [
            agc(o, h, 3, pair_of(o, h, 0, left), dev_right),
            agc(o, h, 4, pair_of(o, h, 1, right), dev_left),
        ]

    def ag3_in(o, h):
        return [
            agc(o, h, 3, pair_of(o, h, 0, opp), dev_left),
            agc(o, h, 4, pair_of(o, h, 1, opp), dev_right),
        ]

    def start(copies):
        for c in copies:
            c.start()

    def recv(copies):
        for c in copies:
            c.wait_recv()

    def sent(copies):
        for c in copies:
            c.wait_send()

    def z_copy(dz, h):
        return rcopy(ag.at[z, h, :, r], ag.at[z, h, :, r], zs.at[dz, h], zr.at[z, h], {"seq": s + dz * PLANE})

    def up_copy(o, h):
        return rcopy(ag.at[o, h], ag.at[o, h], zl_s.at[0, h], zl_r.at[0, h], dev_up)

    def up2_copy(o, h):
        return rcopy(ag.at[o, h], ag.at[o, h], zl_s.at[2, h], zl_r.at[2, h], dev_up)

    def wrap_copy(o, h):
        return rcopy(ag.at[o, h], ag.at[o, h], zl_s.at[1, h], zl_r.at[1, h], dev_top)

    for h in range(heads):
        for dz in range(3, nz - 1):
            @pl.when(z + dz < nz)
            def _(dz=dz, h=h):
                z_copy(dz, h).start()

    m[...] = jnp.full_like(m, -1e30)
    l[...] = jnp.zeros_like(l)
    acc[...] = jnp.zeros_like(acc)
    dqt[...] = jnp.zeros_like(dqt)
    for c in loads[3:]:
        c.wait()
    for w, p in around[n_kv - 1 :]:
        sum_copy(w, p, w, p).wait_recv()
    for h in range(heads):
        @pl.when(has_up)
        def _(h=h):
            up_copy(z, h).start()

        if wrap:
            @pl.when(is_bottom)
            def _(h=h):
                wrap_copy(z, h).start()

    for p in peers:
        start(kv_copies(p, k))

    plane_keys = PLANE * blk

    def forward(c, h, slope, offset, masked):
        kk = ag[c, h, 0].reshape(plane_keys, HD)
        vv = ag[c, h, 1].reshape(plane_keys, HD)
        score = dot(q[h], kk, NT) * LOG2_SCALE
        tiles = [score[:, j * HD : j * HD + HD] for j in range(plane_keys // HD)]
        if masked:
            row = lax.broadcasted_iota(jnp.int32, (tok, 1), 0) * slope + offset
            lane = lax.broadcasted_iota(jnp.int32, (tok, HD), 1)
            tiles = [jnp.where(lane + j * HD <= row, t, -jnp.inf) for j, t in enumerate(tiles)]
        top = functools.reduce(jnp.maximum, tiles)
        m_old = m[h]
        m_new = jnp.maximum(m_old, jnp.max(top, axis=1, keepdims=True))
        alpha = jnp.exp2(m_old - m_new)
        weights = [jnp.exp2(t - m_new) for t in tiles]
        l[h] = l[h] * alpha + functools.reduce(jnp.add, weights)
        w = jnp.concatenate([t.astype(BF16) for t in weights], axis=1)
        acc[h] = acc[h] * alpha + dot(w, vv, NN)
        m[h] = m_new

    def out_copy(src, dst, send, recv_, i, p, slot, h):
        return rcopy(
            src.at[h], dst.at[:, head_cols(slot, h)], send.at[i, h], recv_.at[i, h], {"kv": p}
        )

    def pass_on(dst, send, recv_, slot, h):
        ref = dst.at[:, head_cols(slot, h)]
        return rcopy(ref, ref, send.at[2, h], recv_.at[2, h], {"kv": sibling})

    def out_own(src, dst, i, h):
        return pltpu.make_async_copy(src.at[h], dst.at[:, head_cols(k, h)], loc_sem.at[i + h])

    def out_start(src, dst, send, recv_, i, h):
        out_copy(src, dst, send, recv_, 1, across, k, h).start()
        out_copy(src, dst, send, recv_, 0, sibling, k, h).start()
        out_own(src, dst, i, h).start()

    def out_forward(src, dst, send, recv_, i, h):
        out_copy(src, dst, send, recv_, 1, across, across, h).wait_recv()
        pass_on(dst, send, recv_, across, h).start()

    def out_finish(src, dst, send, recv_, i, h):
        out_own(src, dst, i, h).wait()
        out_copy(src, dst, send, recv_, 0, sibling, sibling, h).wait_recv()
        pass_on(dst, send, recv_, corner, h).wait_recv()
        for slot, p in ((0, sibling), (1, across)):
            out_copy(src, dst, send, recv_, slot, p, k, h).wait_send()
        pass_on(dst, send, recv_, across, h).wait_send()

    att_args = (att, att_out, att_s, att_r, 5)
    dq_args = (dq, dq_out, dq_s, dq_r, 7)

    def far_unit(u):
        h = jnp.where(u >= far, 1, 0)
        return z - (3 + u - h * far), h

    over_at = [jnp.minimum(done + 2, ends[0]), jnp.minimum(done + 3, ends[1])]

    def fwd_step(it):
        @pl.when(it < 2 * far)
        def _():
            o, h = far_unit(it)
            rcopy(ag.at[o, h, :, r], ag.at[o, h, :, r], zs.at[0, h], zr.at[o, h], dev_y).wait_recv()
            start(ag1(o, h))

        @pl.when((it >= LAG) & (it - LAG < 2 * far))
        def _():
            o, h = far_unit(it - LAG)
            recv(ag1_in(o, h))
            start(ag2(o, h))

        @pl.when((it >= 2 * LAG) & (it - 2 * LAG < 2 * far))
        def _():
            o, h = far_unit(it - 2 * LAG)
            recv(ag2_in(o, h))
            start(ag3(o, h))

        @pl.when(it < 4)
        def _():
            local = it >= 2

            @pl.when(it == 2)
            def _():
                for c in own_kv:
                    c.wait()
                for p in peers:
                    recv(kv_copies(p, p))

            forward(
                jnp.where(local, nz, z),
                it % 2,
                jnp.where(local, 1, 0),
                jnp.where(local, 0, r * blk - 1),
                True,
            )

        @pl.when(((it == done - 1) | (it == done)) & has_down)
        def _():
            h = it - (done - 1)
            up_copy(z - 1, h).wait_recv()

            @pl.when(has_up)
            def _():
                up2_copy(z - 1, h).start()

        def chunk(j, _):
            o, h = far_unit(it - 3 * LAG)
            inner = (j == 0) & (it >= 3 * LAG) & (it - 3 * LAG < 2 * far)
            later = jnp.where(j == 1, done + 1, jnp.where(j == 2, over_at[1], ends[1]))
            second = jnp.where(it == later, 1, 0)
            second_below = (j == 3) & ((it == ends[0]) | (it == ends[1])) & (z >= 2)
            below = (j == 1) & ((it == done) | (it == done + 1)) & has_down
            over = (j == 2) & ((it == over_at[0]) | (it == over_at[1])) & is_top & wrap

            @pl.when(inner)
            def _():
                recv(ag3_in(o, h))

            @pl.when(second_below)
            def _():
                up2_copy(z - 2, second).wait_recv()

            if wrap:
                @pl.when(over)
                def _():
                    wrap_copy(0, second).wait_recv()

            @pl.when(inner | below | over | second_below)
            def _():
                forward(
                    jnp.where(j == 0, o, jnp.where(j == 1, z - 1, jnp.where(j == 2, 0, z - 2))), jnp.where(j == 0, h, second), 0, 0, False
                )

            return 0

        lax.fori_loop(0, 4, chunk, 0)

        @pl.when((it == ends[0]) | (it == ends[1]))
        def _():
            h = jnp.where(it == ends[1], 1, 0)
            total = jnp.sum(l[h], axis=1, keepdims=True)
            out = (acc[h] / total).astype(BF16)
            att[h] = out
            delta = jnp.sum(out.astype(F32) * do[h].astype(F32), axis=1, keepdims=True)
            lse_row[h] = jnp.transpose(m[h] + jnp.log2(total))[:8]
            delta_row[h] = jnp.transpose(jnp.broadcast_to(delta, (tok, HD)))[:8]
            out_start(*att_args, h)

    def backward(c, h, slope, offset, masked):
        tile_blocks = KEY_TILE // blk
        lse = lse_row[h, 0:1, :]
        delta = delta_row[h, 0:1, :]
        qh, doh = q[h], do[h]
        for t in range(plane_keys // KEY_TILE):
            bs = slice(t * tile_blocks, (t + 1) * tile_blocks)
            kk = ag[c, h, 0, bs].reshape(KEY_TILE, HD)
            vv = ag[c, h, 1, bs].reshape(KEY_TILE, HD)
            prob = jnp.exp2(dot(kk, qh, NT) * LOG2_SCALE - lse)
            if masked:
                row = lax.broadcasted_iota(jnp.int32, (1, tok), 1) * slope + offset
                key = lax.broadcasted_iota(jnp.int32, (KEY_TILE, tok), 0) + t * KEY_TILE
                prob = jnp.where(key <= row, prob, 0.0)
            ds = (prob * (dot(vv, doh, NT) - delta)).astype(BF16)
            grad[c, h, 1, bs] = dot(prob.astype(BF16), doh, NN).reshape(tile_blocks, blk, HD)
            grad[c, h, 0, bs] = (dot(ds, qh, NN) * SCALE).reshape(tile_blocks, blk, HD)
            dqt[h] += dot(kk, ds, TN)

    def rsc(o, h, i, src, dst, dev):
        return rcopy(src, dst, rs_s.at[o, h, i], rs_r.at[o, h, i], dev)

    def rs1(o, h):
        return [
            rsc(o, h, 0, s1.at[o, h, 0], r1.at[o, h, 0], dev_left),
            rsc(o, h, 1, s1.at[o, h, 1], r1.at[o, h, 1], dev_right),
        ]

    def rs2(o, h):
        return [
            rsc(o, h, 2, s2.at[o, h, 0], r2.at[o, h, 0], dev_left),
            rsc(o, h, 3, s2.at[o, h, 1], r2.at[o, h, 1], dev_right),
        ]

    def rs3(o, h):
        return [rsc(o, h, 4, s3.at[o, h], r3.at[o, h], dev_y)]

    def gz_copy(o, h):
        return rcopy(sz.at[o, h], rz.at[z, h], gz_s.at[o, h], gz_r.at[z, h], {"seq": o * PLANE + r})

    def down_copy(h):
        return rcopy(szl.at[0, h], rzl.at[0, h], gl_s.at[0, h], gl_r.at[0, h], dev_down)

    def down2_copy(h):
        return rcopy(szl.at[2, h], rzl.at[2, h], gl_s.at[2, h], gl_r.at[2, h], dev_down)

    def around_copy(h):
        return rcopy(szl.at[1, h], rzl.at[1, h], gl_s.at[1, h], gl_r.at[1, h], dev_bottom)

    def two(xx):
        return pl.ds(xx * 2, 2)

    def reduce1(o, h):
        s1[o, h, 0] = grad[o, h, 0, two(opp)].astype(BF16)
        s1[o, h, 1] = grad[o, h, 1, two(opp)].astype(BF16)
        start(rs1(o, h))

    def reduce2(o, h):
        recv(rs1(o, h))
        s2[o, h, 0, 0] = (grad[o, h, 0, two(left)] + r1[o, h, 0].astype(F32)).astype(BF16)
        s2[o, h, 0, 1] = grad[o, h, 1, two(left)].astype(BF16)
        s2[o, h, 1, 0] = grad[o, h, 0, two(right)].astype(BF16)
        s2[o, h, 1, 1] = (grad[o, h, 1, two(right)] + r1[o, h, 1].astype(F32)).astype(BF16)
        start(rs2(o, h))

    def summed(o, h, t, yy):
        return grad[o, h, t, x * 2 + yy] + (r2[o, h, 0, t, yy].astype(F32) + r2[o, h, 1, t, yy].astype(F32))

    def reduce3(o, h):
        recv(rs2(o, h))
        for t in range(2):
            s3[o, h, t] = summed(o, h, t, yo).astype(BF16)
        start(rs3(o, h))

    def reduce4(o, h):
        recv(rs3(o, h))
        for t in range(2):
            sz[o, h, t] = (summed(o, h, t, y) + r3[o, h, t].astype(F32)).astype(BF16)
        gz_copy(o, h).start()

    def d0_copy(w, slot, h):
        return rcopy(s0.at[h, w], r0.at[h, slot], d0_s.at[h, w], d0_r.at[h, slot], {"seq": base + w})

    def fin_copy(h, t, p, slot):
        return rcopy(
            fin.at[h, t, :, part(p)],
            fin_in.at[t, :, :, head_cols(slot, h)],
            fin_s.at[h, t, p],
            fin_r.at[h, t, slot],
            {"kv": p},
        )

    def own_fin(h, t):
        return pltpu.make_async_copy(
            fin.at[h, t, :, part(k)], fin_in.at[t, :, :, head_cols(k, h)], loc_sem.at[9 + 2 * h + t]
        )

    def far_grad(g):
        h = jnp.where(g >= z, 1, 0)
        j = g - h * z
        next_at = jnp.minimum(z - 1, 5)
        furthest = j - 1 - jnp.where(j > next_at, 1, 0)
        furthest = jnp.where(is_top, jnp.where(furthest == z - 3, 0, furthest + 1), furthest)
        return jnp.where(j == next_at, z - 1, jnp.where(j == 0, z - 2, furthest)), h

    def in_plane(g):
        o, _ = far_grad(g)
        return (g >= 0) & (g < 2 * z) & (z - o >= 3) & jnp.logical_not(is_top & (o == 0))

    def bwd_step(g):
        o, h = far_grad(g)

        @pl.when(g < 2 * z)
        def _():
            backward(o, h, 0, 0, False)

            @pl.when(o == z - 2)
            def _():
                szl[2, h] = grad[o, h].astype(BF16)
                down2_copy(h).start()

            @pl.when(o == z - 1)
            def _():
                @pl.when(has_up)
                def _():
                    down2_copy(h).wait_recv()
                    grad[z - 1, h] += rzl[2, h].astype(F32)

                szl[0, h] = grad[z - 1, h].astype(BF16)
                down_copy(h).start()

            @pl.when((o == 0) & is_top)
            def _():
                szl[1, h] = grad[0, h].astype(BF16)
                around_copy(h).start()

        @pl.when(in_plane(g))
        def _():
            reduce1(o, h)

        @pl.when((g >= 2 * z) & (g < 2 * z + 4))
        def _():
            n = g - 2 * z
            head, local = n // 2, (n == 1) | (n == 2)
            backward(
                jnp.where(local, nz, z), head, jnp.where(local, 1, 0), jnp.where(local, 0, r * blk - 1), True
            )

            @pl.when(n % 2 == 1)
            def _():
                dq[head] = jnp.transpose(dqt[head] * SCALE).astype(BF16)
                out_start(*dq_args, head)

            @pl.when(local)
            def _():
                fin[head] = grad[nz, head].astype(BF16)
                for t in range(2):
                    own_fin(head, t).start()
                    for p in peers:
                        fin_copy(head, t, p, k).start()

            @pl.when(jnp.logical_not(local))
            def _():
                @pl.when(has_up)
                def _():
                    down_copy(head).wait_recv()
                    grad[z, head] += rzl[0, head].astype(F32)

                if wrap:
                    @pl.when(is_bottom)
                    def _():
                        around_copy(head).wait_recv()
                        grad[z, head] += rzl[1, head].astype(F32)

                for w in range(PLANE):
                    for t in range(2):
                        s0[head, w, t] = grad[z, head, t, w].astype(BF16)
                for w in mates:
                    d0_copy(w, r, head).start()

        for back, stage in ((3, reduce4), (2, reduce3), (1, reduce2)):
            @pl.when(in_plane(g - back * LAG))
            def _(back=back, stage=stage):
                stage(*far_grad(g - back * LAG))

    last_it = bwd_at + 2 * z + 3 * LAG - 1

    def step(it, _):
        @pl.when(it <= ends[1])
        def _():
            fwd_step(it)

        @pl.when(it >= bwd_at)
        def _():
            bwd_step(it - bwd_at)

        for h in range(heads):
            @pl.when(it == ends[h] + 4)
            def _(h=h):
                out_forward(*att_args, h)

        @pl.when(it == last_it)
        def _():
            out_forward(*dq_args, 0)

        return 0

    lax.fori_loop(0, last_it + 1, step, 0)
    out_forward(*dq_args, 1)
    for h in range(heads):
        for w in mates:
            d0_copy(w, w, h).wait_recv()
        for t in range(2):
            own[h, t] = functools.reduce(jnp.add, [r0[h, w, t].astype(F32) for w in mates], grad[z, h, t, r])

    def add_plane(o, _):
        for h in range(heads):
            rcopy(sz.at[0, h], rz.at[o, h], gz_s.at[0, h], gz_r.at[o, h], dev_y).wait_recv()
        own[...] += rz[o].astype(F32)
        return 0

    lax.fori_loop(z + 3, jnp.where(is_bottom, nz - 1, nz), add_plane, 0)
    tail[...] = own[...].astype(BF16)

    def tail_copy(p, slot):
        return rcopy(
            tail.at[:, :, part(p)],
            tail_in.at[pl.ds(slot * heads, heads)],
            tail_s.at[p],
            tail_r.at[slot],
            {"kv": p},
        )

    for p in peers:
        tail_copy(p, k).start()
    own_tail = pltpu.make_async_copy(
        tail.at[:, :, part(k)], tail_in.at[pl.ds(k * heads, heads)], loc_sem.at[13]
    )
    own_tail.start()
    for w, p in around:
        sum_copy(w, p, r, k).wait_send()
    for p in peers:
        sent(kv_copies(p, k))

    def sent_head(h, _):
        for dz in range(3, nz - 1):
            @pl.when(z + dz < nz)
            def _(dz=dz):
                z_copy(dz, h).wait_send()

        @pl.when(has_up)
        def _():
            up_copy(z, h).wait_send()

        @pl.when(has_up & has_down)
        def _():
            up2_copy(z - 1, h).wait_send()

        @pl.when(has_down)
        def _():
            down_copy(h).wait_send()

        @pl.when(z >= 2)
        def _():
            down2_copy(h).wait_send()

        if wrap:
            @pl.when(is_bottom)
            def _():
                wrap_copy(z, h).wait_send()

            @pl.when(is_top)
            def _():
                around_copy(h).wait_send()

        def sent_plane(o, _):
            direct = (z - o >= 3) & jnp.logical_not((o == 0) & is_top)

            @pl.when(direct)
            def _():
                sent(ag1(o, h) + ag2(o, h) + ag3(o, h) + rs1(o, h) + rs2(o, h) + rs3(o, h))
                gz_copy(o, h).wait_send()

            return 0

        for w in mates:
            d0_copy(w, r, h).wait_send()
        lax.fori_loop(0, z, sent_plane, 0)
        return 0

    lax.fori_loop(0, heads, sent_head, 0)
    for h in range(heads):
        out_finish(*att_args, h)
        out_finish(*dq_args, h)
    for h in range(heads):
        for t in range(2):
            own_fin(h, t).wait()
            for p in peers:
                fin_copy(h, t, p, p).wait_recv()
    own_tail.wait()
    for p in peers:
        tail_copy(p, p).wait_recv()
    results = [
        pltpu.make_async_copy(res.at[t], ref, loc_sem.at[14 + t]) for t, ref in enumerate((dk_out, dv_out))
    ]
    for t in range(2):
        arrived = jnp.concatenate([tail_in[h, t].astype(F32) for h in range(n_kv * heads)], axis=1)
        for b in range(blocks):
            res[t, b] = (fin_in[t, b].astype(F32) + jnp.where(summary == b, arrived, 0.0)).astype(BF16)
        results[t].start()

    for p in peers:
        tail_copy(p, k).wait_send()
        for h in range(heads):
            for t in range(2):
                fin_copy(h, t, p, k).wait_send()
    for c in results:
        c.wait()


def hand_over(*refs):
    n = (len(refs) - 2) // 3
    ins, outs, held = refs[:n], refs[n : 2 * n], refs[2 * n : 3 * n]
    load_sem, save_sem = refs[3 * n :]
    loads = [pltpu.make_async_copy(a, b, load_sem.at[i]) for i, (a, b) in enumerate(zip(ins, held))]
    saves = [pltpu.make_async_copy(a, b, save_sem.at[i]) for i, (a, b) in enumerate(zip(held, outs))]
    for c in loads:
        c.start()
    for load, save in zip(loads, saves):
        load.wait()
        save.start()
    for c in saves:
        c.wait()


def shards(queries, keys, values, layout, grad_out):
    tok, feat = queries.shape
    blocks, part_tok = keys.shape[0], keys.shape[1]
    n_kv = lax.axis_size("kv")
    nz = lax.axis_size("seq") // PLANE
    blk = part_tok * n_kv
    width = feat // n_kv
    heads = width // HD
    dma = pltpu.SemaphoreType.DMA

    def vm(*shape, dtype=BF16):
        return pltpu.VMEM(shape, dtype)

    results = tuple(jax.ShapeDtypeStruct(a.shape, BF16) for a in (queries, queries, keys, keys))
    hbm = [pl.BlockSpec(memory_space=pltpu.HBM)]
    made = pl.pallas_call(
        functools.partial(kernel, nz),
        out_shape=results,
        in_specs=hbm * 5,
        out_specs=hbm * 4,
        scratch_shapes=[
            vm(layout.shape[1], min(128, layout.shape[0]), dtype=jnp.int32),
            vm(*keys.shape),
            vm(*keys.shape),
            vm(heads, tok, HD),
            vm(heads, tok, HD),
            vm(n_kv * heads, 2, part_tok, HD),
            vm(nz + 1, heads, 2, PLANE, blk, HD),
            vm(nz + 1, heads, 2, PLANE, blk, HD, dtype=F32),
            vm(heads, tok, HD, dtype=F32),
            vm(heads, tok, HD, dtype=F32),
            vm(heads, tok, HD, dtype=F32),
            vm(heads, 8, tok, dtype=F32),
            vm(heads, 8, tok, dtype=F32),
            vm(heads, HD, tok, dtype=F32),
            vm(heads, tok, HD),
            vm(heads, tok, HD),
            vm(heads, 2, blocks, blk, HD),
            vm(2, blocks, part_tok, feat),
            vm(heads, 2, blk, HD),
            vm(n_kv * heads, 2, part_tok, HD),
            vm(2, blocks, part_tok, feat),
            vm(heads, PLANE, 2, blk, HD),
            vm(nz, heads, 2, 2, blk, HD),
            vm(nz, heads, 2, 2, 2, blk, HD),
            vm(nz, heads, 2, blk, HD),
            vm(nz, heads, 2, blk, HD),
            vm(3, heads, 2, PLANE, blk, HD),
            vm(heads, PLANE, 2, blk, HD),
            vm(nz, heads, 2, 2, blk, HD),
            vm(nz, heads, 2, 2, 2, blk, HD),
            vm(nz, heads, 2, blk, HD),
            vm(nz, heads, 2, blk, HD),
            vm(3, heads, 2, PLANE, blk, HD),
            vm(heads, 2, blk, HD, dtype=F32),
            dma((3 + 2 * heads,)),
            dma((PLANE, n_kv)),
            dma((PLANE, n_kv)),
            dma((heads, 2, n_kv)),
            dma((heads, 2, n_kv)),
            dma((nz, heads)),
            dma((nz, heads)),
            dma((3, heads)),
            dma((3, heads)),
            dma((nz, heads, 5)),
            dma((nz, heads, 5)),
            dma((nz, heads, 5)),
            dma((nz, heads, 5)),
            dma((nz, heads)),
            dma((nz, heads)),
            dma((3, heads)),
            dma((3, heads)),
            dma((3, heads)),
            dma((3, heads)),
            dma((3, heads)),
            dma((3, heads)),
            dma((heads, 2, n_kv)),
            dma((heads, 2, n_kv)),
            dma((n_kv,)),
            dma((n_kv,)),
            dma((heads, PLANE)),
            dma((heads, PLANE)),
            dma((16,)),
        ],
        compiler_params=pltpu.CompilerParams(
            collective_id=0, has_side_effects=True, vmem_limit_bytes=VMEM_LIMIT
        ),
    )(layout.T, queries, keys, values, grad_out)
    return pl.pallas_call(
        hand_over,
        out_shape=results,
        in_specs=hbm * 4,
        out_specs=hbm * 4,
        scratch_shapes=[*(vm(*a.shape) for a in results), dma((4,)), dma((4,))],
        compiler_params=pltpu.CompilerParams(vmem_limit_bytes=VMEM_LIMIT),
    )(*made)


def solution(mesh):
    return jax.shard_map(
        shards,
        mesh=mesh,
        in_specs=(P("seq", None), P("seq", "kv", None), P("seq", "kv", None), P(), P("seq", None)),
        out_specs=(P("seq", None), P("seq", None), P("seq", "kv", None), P("seq", "kv", None)),
        check_vma=False,
    )
```
